512 devices in a mesh: tm: 32 (over z_hi, x, core), space: 16 (over y, z_lo).
Axes of the slice: x: 4, y: 8, z: 8 (z_hi: 4, z_lo: 2; z = z_hi * 2 + z_lo), core: 2. Of those that a mesh axis runs over, the one named last changes fastest.
Arguments:
- initial_density: float32 [384, 512], P('space'), may hold values from 0.5 to 2
- terminal_cost: float32 [384, 512], P('space'), may hold values from -1.2 to 1.2
- running_cost: float32 [384, 512], P('space'), may hold values from -0.3 to 0.3
- discount_rate: float32 [384, 512], P('space'), may hold values from 0.003 to 0.5
- slice_steps: int32 [32], replicated, may hold values from 4 to 8
Outputs:
- density_path: float32 [32, 384, 512], P('tm', 'space')
- value_path: float32 [32, 384, 512], P('tm', 'space')
The draws below stay inside these ranges and needn't reach their ends.
All inputs are finite; a program needn't handle non-finite values.
Results may differ from the reference program's by a relative error of at most 0.0003.
Values sent between devices are 32-bit elements; how exact they have to be, the bound alone decides.
No kernel may reach another device: no remote copies, remote signals or barrier semaphores. Data moves between devices by JAX's collectives and lax.ppermute only.
A program may use at most 64 MiB of HBM per device.

```python
import math
import jax
import jax.numpy as jnp
from jax import lax

NY = 512
K = 8
ITERS = 2
SLICES = 32
NX = 384


def plant(array, stream_key, least, high):
    extent = array.shape
    index_at = [jax.random.randint(jax.random.fold_in(stream_key, axis), (), 0, extent[axis]) for axis in range(len(extent))]
    array = array.at[tuple(index_at)].set(least)
    longest = extent.index(max(extent))
    index_at[longest] = (index_at[longest] + 1) % extent[longest]
    return array.at[tuple(index_at)].set(high)


def block_levels(rng, shape, cuts, low, top_value):
    level = 1.0
    for dim, blocks in cuts:
        steps = jax.random.uniform(jax.random.fold_in(jax.random.fold_in(rng, 6), dim), (blocks,), jnp.float32, low / len(cuts), top_value / len(cuts))
        level = level * jnp.repeat(jnp.exp(steps), shape[dim] // blocks).reshape((-1,) + (1,) * (len(shape) - 1 - dim))
    return level


def gaussian(key, extent, spread, most, split=(), dtype=jnp.bfloat16):
    loudness = block_levels(key, extent, split, -0.22, 0.18) if split else 1.0
    drawn = jax.random.normal(key, extent, jnp.float32) * spread * loudness
    return jnp.minimum(jnp.maximum(drawn, -most), most).astype(dtype)


def setup_inputs(seed: int = 0) -> dict:
    splits = jax.random.split(jax.random.key(seed), 6)
    return {
        "initial_density": jnp.clip(jnp.exp(math.log(2.0) - 1.3862944 * jax.random.uniform(splits[0], (NX, NY), jnp.float32) ** block_levels(splits[0], (NX, NY), ((0, 16),), -0.2, 0.2)), 0.5, 2.0),
        "terminal_cost": gaussian(splits[1], (NX, NY), 0.2, 1.2, ((0, 16),), jnp.float32),
        "running_cost": gaussian(splits[2], (NX, NY), 0.05, 0.3, ((0, 16),), jnp.float32),
        "discount_rate": jnp.clip(jnp.exp(math.log(0.5) - 5.115996 * jax.random.uniform(splits[3], (NX, NY), jnp.float32) ** block_levels(splits[3], (NX, NY), ((0, 16),), -0.2, 0.2)), 0.003, 0.5),
        "slice_steps": plant(jax.random.randint(splits[4], (SLICES,), 4, K + 1), jax.random.fold_in(splits[4], 1), 4, K).astype(jnp.int32),
    }


time_step = 0.05
diffusion = 2.0
coupling = 0.1


def laplace(padded):
    middle = padded[1:-1]
    return padded[2:] + padded[:-2] + jnp.roll(middle, 1, 1) + jnp.roll(middle, -1, 1) - 4.0 * middle


def slopes(padded):
    middle = padded[1:-1]
    return 0.5 * (padded[2:] - padded[:-2]), 0.5 * (jnp.roll(middle, -1, 1) - jnp.roll(middle, 1, 1))


def value_step(padded, source):
    slope_across, slope_along = slopes(padded)
    hamilton = 0.5 * (slope_across * slope_across + slope_along * slope_along)
    return padded[1:-1] + time_step * (diffusion * laplace(padded) - hamilton + source)


def density_step(density, value):
    slope_across, slope_along = slopes(value)
    flux_across = density * slope_across
    flux_along = density * slope_along
    inner = flux_along[1:-1]
    divergence = 0.5 * (flux_across[2:] - flux_across[:-2]) + 0.5 * (jnp.roll(inner, -1, 1) - jnp.roll(inner, 1, 1))
    return density[1:-1] + time_step * (diffusion * laplace(density) + divergence)


def wrap_rows(field, width):
    return jnp.concatenate([field[-width:], field, field[:width]], axis=0)


def fine_solve(density_start, value_end, running_cost, steps):
    source = running_cost + coupling * density_start
    value_now = value_end
    stored = [value_now]
    for substep in range(K):
        active = substep >= K - steps
        value_now = jnp.where(active, value_step(wrap_rows(value_now, 1), source), value_now)
        stored.append(value_now)
    density_now = density_start
    for substep in range(K):
        active = substep < steps
        density_now = jnp.where(active, density_step(wrap_rows(density_now, 1), wrap_rows(stored[K - substep], 2)), density_now)
    return density_now, value_now


def reference(initial_density, terminal_cost, running_cost, discount_rate, slice_steps):
    steps_float = slice_steps.astype(jnp.float32)
    factors = [jnp.exp(-discount_rate * (time_step * steps_float[number])) for number in range(SLICES)]
    reliefs = [-jnp.expm1(-discount_rate * (time_step * steps_float[number])) / discount_rate * running_cost for number in range(SLICES)]
    densities = [initial_density]
    for number in range(SLICES - 1):
        densities.append(factors[number] * densities[number])
    values = [terminal_cost] * SLICES
    for number in range(SLICES - 2, -1, -1):
        values[number] = factors[number + 1] * values[number + 1] + reliefs[number + 1]
    for iteration in range(ITERS):
        fine_density, fine_value = lax.map(
            lambda item: fine_solve(item[0], item[1], running_cost, item[2]),
            (jnp.stack(densities), jnp.stack(values), slice_steps))
        density_terms = [fine_density[number] - factors[number] * densities[number] for number in range(SLICES)]
        value_terms = [fine_value[number] - factors[number] * values[number] for number in range(SLICES)]
        new_densities = [initial_density]
        for number in range(SLICES - 1):
            new_densities.append(factors[number] * new_densities[number] + density_terms[number])
        new_values = [terminal_cost] * SLICES
        for number in range(SLICES - 2, -1, -1):
            new_values[number] = factors[number + 1] * new_values[number + 1] + value_terms[number + 1]
        densities = new_densities
        values = new_values
    return jnp.stack(densities), jnp.stack(values)
```

```python
import jax
import jax.numpy as jnp
from jax import lax
from jax.experimental import pallas as pl
from jax.experimental.pallas import tpu as pltpu
from jax.sharding import Mesh
from jax.sharding import PartitionSpec as P


K = 8
SLICES = 32
LEAST = 4
KINDS = K - LEAST + 1
TM = ("zh", "x", "c")
SPACE = ("y", "zl")

time_step = 0.05
diffusion = 2.0
coupling = 0.1

ROWS = 24
TILE_ROWS = 12
TILE_COLS = 32
LANES = 128
COL_AT = 48
FRAME1 = 88
FRAME2 = 56
SCALE = 16.0


def planes_of(ref, at, start, count):
    return [ref[(*at, pl.ds(start + k, 8, stride=count), slice(None))] for k in range(count)]


def put_planes(ref, at, start, planes):
    count = len(planes)
    for k, plane in enumerate(planes):
        ref[(*at, pl.ds(start + k, 8, stride=count), slice(None))] = plane


def row_above(planes):
    return [pltpu.roll(planes[-1], 1, 0), *planes[:-1]]


def row_below(planes):
    return [*planes[1:], pltpu.roll(planes[0], 7, 0)]


def left(plane):
    return pltpu.roll(plane, 1, 1)


def right(plane):
    return pltpu.roll(plane, LANES - 1, 1)


def slope_planes(planes):
    up, down = row_above(planes), row_below(planes)
    slopes, sums = [], []
    for k, plane in enumerate(planes):
        west, east = left(plane), right(plane)
        slopes.append((down[k] - up[k], east - west))
        sums.append((up[k] + down[k]) + (west + east))
    return slopes, sums


def fine_pairs(order, steps, values, densities, cost, sources, across, along, out_value, out_density, spots):
    (value_at, value_n), (density_at, density_n) = spots

    def pair(number, carry):
        own = [order[2 * number], order[2 * number + 1]]
        trips = [steps[own[0]], steps[own[1]]]
        most = jnp.maximum(trips[0], trips[1])
        start = []
        for h in range(2):
            start.append(planes_of(values, (own[h],), value_at, value_n))
            held = planes_of(densities, (own[h],), value_at, value_n)
            for k in range(value_n):
                sources[h, k] = cost[k] + (0.5 / SCALE * coupling) * held[k]

        def put_slopes(h, q, slopes):
            put_planes(across, (h, q), value_at, [a for a, _ in slopes])
            put_planes(along, (h, q), value_at, [b for _, b in slopes])

        def value_step(q, now):
            result = []
            for h in range(2):
                active = q >= most - trips[h]
                keep = jnp.where(active, 1.0 - 4.0 * time_step * diffusion, 1.0)
                share = jnp.where(active, time_step * diffusion, 0.0)
                slopes, sums = slope_planes(now[h])
                put_slopes(h, q, slopes)
                result.append([
                    keep * plane + share * (sums[k] + (sources[h, k] - (slopes[k][0] * slopes[k][0] + slopes[k][1] * slopes[k][1])))
                    for k, plane in enumerate(now[h])
                ])
            return result

        now = lax.fori_loop(0, most, value_step, start)
        for h in range(2):
            put_slopes(h, most, slope_planes(now[h])[0])
            put_planes(out_value, (own[h],), value_at, now[h])

        def density_step(i, held):
            q = most - i
            result = []
            for h in range(2):
                active = i < trips[h]
                keep = jnp.where(active, 1.0 - 4.0 * time_step * diffusion, 1.0)
                share = jnp.where(active, time_step * diffusion, 0.0)
                a = planes_of(across, (h, q), density_at, density_n)
                b = planes_of(along, (h, q), density_at, density_n)
                here = held[h]
                twice = [plane + plane for plane in here]
                flux = [twice[k] * a[k] for k in range(density_n)]
                below = row_below([here[k] + flux[k] for k in range(density_n)])
                above = row_above([here[k] - flux[k] for k in range(density_n)])
                new = []
                for k in range(density_n):
                    drift = twice[k] * b[k]
                    around = (below[k] + above[k]) + (right(here[k] + drift) + left(here[k] - drift))
                    new.append(keep * here[k] + share * around)
                result.append(new)
            return result

        begin = [planes_of(densities, (own[h],), density_at, density_n) for h in range(2)]
        end = lax.fori_loop(0, most, density_step, begin)
        for h in range(2):
            put_planes(out_density, (own[h],), density_at, end[h])
        return carry

    lax.fori_loop(0, SLICES // 2, pair, 0)


def main_kernel(order, steps, core, own, low, high, far, message, field, factors, reliefs, cost, m0, u0, m1, u1, fm, fu, across, along, sources):
    for part in range(4):

        @pl.when(core[0] == 0)
        def _(part=part):
            field[part, 6:16] = far[part, 6:16]
            field[part, 16:40] = low[part]
            field[part, 40:64] = own[part]
            field[part, 64:86] = high[part, 0:22]

        @pl.when(core[0] != 0)
        def _(part=part):
            field[part, 6:28] = low[part, 2:24]
            field[part, 28:52] = own[part]
            field[part, 52:76] = high[part]
            field[part, 76:86] = far[part, 0:10]

    rate, running = field[3], field[2]
    quotient = running / rate
    for kind in range(KINDS):
        factor = jnp.exp(rate * (-time_step * (LEAST + kind)))
        factors[kind] = factor
        reliefs[kind] = (1.0 - factor) * quotient * (1.0 / SCALE)
    cost[...] = running * (0.5 / SCALE)

    def opening(j, now):
        density, value = now
        back = SLICES - 1 - j
        m0[j] = density
        u0[back] = value
        kind = steps[back] - LEAST
        return factors[steps[j] - LEAST] * density, factors[kind] * value + reliefs[kind]

    lax.fori_loop(0, SLICES, opening, (field[0], field[1] * (1.0 / SCALE)))

    fine_pairs(order, steps, u0, m0, planes_of(cost, (), 6, 10), sources, across, along, fu, fm, ((6, 10), (14, 8)))

    inner = pl.ds(16, FRAME2)

    def first_sweep(j, now):
        density, value = now
        back = SLICES - 1 - j
        m1[j] = density
        u1[back] = value
        density = factors[steps[j] - LEAST, inner] * (density - m0[j, inner]) + fm[j, inner]
        value = factors[steps[back] - LEAST, inner] * (value - u0[back, inner]) + fu[back, inner]
        return density, value

    lax.fori_loop(0, SLICES, first_sweep, (field[0, inner], field[1, inner] * (1.0 / SCALE)))

    fine_pairs(order, steps, u1, m1, planes_of(cost, (), 22, 6), sources, across, along, fu, fm, ((6, 6), (16, 4)))

    tile, wide = pl.ds(24, 16), pl.ds(40, 16)
    lane = lax.broadcasted_iota(jnp.int32, (8, LANES), 1)
    for_density, first_rows = lane < 64, (lane % 64) < 32

    def second_sweep(j, now):
        density, value = now
        back = SLICES - 1 - j
        u0[back, 0:16] = value
        m0[j, 0:16] = density
        density = factors[steps[j] - LEAST, wide] * (density - m1[j, tile]) + fm[j, tile]
        value = factors[steps[back] - LEAST, wide] * (value - u1[back, tile]) + fu[back, tile]
        return density, value

    lax.fori_loop(0, SLICES, second_sweep, (field[0, wide], field[1, wide] * (1.0 / SCALE)))

    def moved(plane, lane_now):
        return pltpu.roll(plane, (lane_now - COL_AT) % LANES, 1)

    def packed(j, carry):
        density = jnp.where(first_rows, moved(m0[j, 0:8], 0), moved(m0[j, 8:16], 32))
        value = SCALE * jnp.where(first_rows, moved(u0[j, 0:8], 64), moved(u0[j, 8:16], 96))
        message[j] = jnp.where(for_density, density, value)
        return carry

    lax.fori_loop(0, SLICES, packed, 0)


def window_kernel(place, *refs):
    blocks, (near, far) = refs[:8], refs[8:]
    shift, first = place[2], place[3]
    lane = lax.broadcasted_iota(jnp.int32, (ROWS, LANES), 1)
    for part in range(4):
        a = pltpu.roll(blocks[2 * part][...], shift, 1)
        b = pltpu.roll(blocks[2 * part + 1][...], shift, 1)
        window = jnp.where(lane < shift, a, b)
        near[part] = window

        @pl.when(first == 0)
        def _(window=window, part=part):
            far[part] = window[8:24]

        @pl.when(first != 0)
        def _(window=window, part=part):
            far[part] = window[0:16]


def gather_kernel(received, density, value):
    lane = lax.broadcasted_iota(jnp.int32, (8, LANES), 1)
    for column in range(4):
        for half in range(2):
            for out, base in ((density, 0), (value, 64)):
                for rows, block, begin in ((8, base, 0), (4, base + 32, 8)):
                    whole = None
                    for x in range(4):
                        source = received[column * 8 + x * 2 + half]
                        piece = pltpu.roll(source, (32 * x - block) % LANES, 1)
                        whole = piece if whole is None else jnp.where(lane >= 32 * x, piece, whole)
                    at = TILE_ROWS * half + begin
                    out[0, at : at + rows, LANES * column : LANES * (column + 1)] = whole[0:rows]


def vmem():
    return pl.BlockSpec(memory_space=pltpu.VMEM)


def smem():
    return pl.BlockSpec(memory_space=pltpu.SMEM)


def f32(*shape):
    return jax.ShapeDtypeStruct(shape, jnp.float32)


def windows(place, arrays):
    specs, operands = [], []
    for array in arrays:
        for which in range(2):
            specs.append(pl.BlockSpec((ROWS, LANES), lambda i, place, which=which: (0, place[which])))
            operands.append(array)
    return pl.pallas_call(
        window_kernel,
        out_shape=[f32(4, ROWS, LANES), f32(4, 16, LANES)],
        grid_spec=pltpu.PrefetchScalarGridSpec(
            num_scalar_prefetch=1,
            grid=(1,),
            in_specs=specs,
            out_specs=[
                pl.BlockSpec((4, ROWS, LANES), lambda i, place: (0, 0, 0)),
                pl.BlockSpec((4, 16, LANES), lambda i, place: (0, 0, 0)),
            ],
        ),
        name="windows",
    )(place, *operands)


def both_iterations(order, steps, core, own, low, high, far):
    scratch = [
        (4, FRAME1, LANES),
        (KINDS, FRAME1, LANES),
        (KINDS, FRAME1, LANES),
        (FRAME1, LANES),
        (SLICES, FRAME1, LANES),
        (SLICES, FRAME1, LANES),
        (SLICES, FRAME2, LANES),
        (SLICES, FRAME2, LANES),
        (SLICES, FRAME1, LANES),
        (SLICES, FRAME1, LANES),
        (2, K + 1, FRAME1, LANES),
        (2, K + 1, FRAME1, LANES),
        (2, 10, 8, LANES),
    ]
    return pl.pallas_call(
        main_kernel,
        out_shape=f32(SLICES, 8, LANES),
        in_specs=[smem(), smem(), smem(), vmem(), vmem(), vmem(), vmem()],
        out_specs=vmem(),
        scratch_shapes=[pltpu.VMEM(shape, jnp.float32) for shape in scratch],
        compiler_params=pltpu.CompilerParams(vmem_limit_bytes=32 * 2**20),
        name="both_iterations",
    )(order, steps, core, own, low, high, far)


def gathered(received):
    return pl.pallas_call(
        gather_kernel,
        out_shape=[f32(1, ROWS, 512), f32(1, ROWS, 512)],
        in_specs=[vmem()],
        out_specs=[vmem(), vmem()],
        name="gathered",
    )(received)


def from_offset(array, offset):
    count = 16
    return lax.ppermute(array, SPACE, [((i + offset) % count, i) for i in range(count)])


def on_device(initial_density, terminal_cost, running_cost, discount_rate, slice_steps):
    core = lax.axis_index("c")
    column = lax.axis_index("zh") * 4 + lax.axis_index("x")
    begin = (column * TILE_COLS - COL_AT) % 512
    first_block = begin // LANES
    shift = (LANES - begin % LANES) % LANES
    whole = (shift == 0).astype(jnp.int32)
    place = jnp.stack([first_block, (first_block + 1 - whole) % 4, shift, core]).astype(jnp.int32)
    own, edge = windows(place, (initial_density, terminal_cost, running_cost, discount_rate))
    low = from_offset(own, -1)
    high = from_offset(own, 1)
    hops = []
    for space in range(16):
        for c in range(2):
            source = (space - 2) % 16 if c == 0 else (space + 2) % 16
            hops.append((c * 16 + source, c * 16 + space))
    far = lax.ppermute(edge, ("c", *SPACE), hops)
    numbers = jnp.arange(SLICES, dtype=jnp.int32)
    ahead = (slice_steps[None, :] < slice_steps[:, None]) | ((slice_steps[None, :] == slice_steps[:, None]) & (numbers[None, :] < numbers[:, None]))
    rank = jnp.sum(ahead.astype(jnp.int32), axis=1)
    order = jnp.sum(jnp.where(rank[None, :] == numbers[:, None], numbers[None, :], 0), axis=1)
    message = both_iterations(order, slice_steps, core[None].astype(jnp.int32), own, low, high, far)
    received = lax.all_to_all(message, TM, 0, 0, tiled=True)
    return tuple(gathered(received))


def solution(mesh):
    finer = Mesh(mesh.devices.reshape(4, 4, 2, 8, 2), ("zh", "x", "c", "y", "zl"))
    placed = (P(SPACE, None), P(SPACE, None), P(SPACE, None), P(SPACE, None), P())
    return jax.shard_map(
        on_device,
        mesh=finer,
        in_specs=placed,
        out_specs=(P(TM, SPACE, None), P(TM, SPACE, None)),
        check_vma=False,
    )
```

```python
import jax
import jax.numpy as jnp
from jax import lax
from jax.experimental import pallas as pl
from jax.experimental.pallas import tpu as pltpu
from jax.sharding import Mesh
from jax.sharding import PartitionSpec as P


K = 8
SLICES = 32
LEAST = 4
KINDS = K - LEAST + 1
GROUP = 8
TM = ("zh", "x", "c")
SPACE = ("y", "zl")

time_step = 0.05
diffusion = 2.0
coupling = 0.1

ROWS = 24
TILE_ROWS = 12
TILE_COLS = 32
LANES = 128
COL_AT = 48
FRAME1 = 88
FRAME2 = 56
SCALE = 16.0


def planes_of(ref, at, start, count):
    return [ref[(*at, pl.ds(start + k, 8, stride=count), slice(None))] for k in range(count)]


def put_planes(ref, at, start, planes):
    count = len(planes)
    for k, plane in enumerate(planes):
        ref[(*at, pl.ds(start + k, 8, stride=count), slice(None))] = plane


def row_above(planes):
    return [pltpu.roll(planes[-1], 1, 0), *planes[:-1]]


def row_below(planes):
    return [*planes[1:], pltpu.roll(planes[0], 7, 0)]


def left(plane):
    return pltpu.roll(plane, 1, 1)


def right(plane):
    return pltpu.roll(plane, LANES - 1, 1)


def slope_planes(planes):
    up, down = row_above(planes), row_below(planes)
    slopes, sums = [], []
    for k, plane in enumerate(planes):
        west, east = left(plane), right(plane)
        slopes.append((down[k] - up[k], east - west))
        sums.append((up[k] + down[k]) + (west + east))
    return slopes, sums


def fine_groups(order, steps, values, densities, cost, sources, across, along, value_now, density_now, out_value, out_density, spots):
    (value_at, value_n), (density_at, density_n) = spots
    keep_all, share_all = 1.0 - 4.0 * time_step * diffusion, time_step * diffusion

    def group(number, carry):
        own = [order[GROUP * number + h] for h in range(GROUP)]
        trips = [steps[j] for j in own]
        most = trips[-1]
        for h in range(GROUP):
            start = planes_of(values, (own[h],), value_at, value_n)
            held = planes_of(densities, (own[h],), value_at, value_n)
            for k in range(value_n):
                value_now[0][h, k] = value_now[1][h, k] = start[k]
                sources[h, k] = cost[k] + (0.5 / SCALE * coupling) * held[k]
            for k, plane in enumerate(planes_of(densities, (own[h],), density_at, density_n)):
                density_now[0][h, k] = plane

        def slopes_of(q, h):
            now = [value_now[q % 2][h, k] for k in range(value_n)]
            slopes, sums = slope_planes(now)
            put_planes(across, (h, q), value_at, [a for a, _ in slopes])
            put_planes(along, (h, q), value_at, [b for _, b in slopes])
            return now, slopes, sums

        def value_step(q):
            for h in range(GROUP):
                keep, share = keep_all, share_all
                if q < K - LEAST:
                    active = q >= K - trips[h]
                    keep, share = jnp.where(active, keep, 1.0), jnp.where(active, share, 0.0)
                now, slopes, sums = slopes_of(q, h)
                for k in range(value_n):
                    a, b = slopes[k]
                    value_now[1 - q % 2][h, k] = keep * now[k] + share * (sums[k] + (sources[h, k] - (a * a + b * b)))

        def density_step(i):
            for h in range(GROUP):
                keep, share = keep_all, share_all
                if i >= LEAST:
                    active = i < trips[h]
                    keep, share = jnp.where(active, keep, 1.0), jnp.where(active, share, 0.0)
                a = planes_of(across, (h, K - i), density_at, density_n)
                b = planes_of(along, (h, K - i), density_at, density_n)
                here = [density_now[i % 2][h, k] for k in range(density_n)]
                twice = [plane + plane for plane in here]
                flux = [twice[k] * a[k] for k in range(density_n)]
                below = row_below([here[k] + flux[k] for k in range(density_n)])
                above = row_above([here[k] - flux[k] for k in range(density_n)])
                for k in range(density_n):
                    drift = twice[k] * b[k]
                    around = (below[k] + above[k]) + (right(here[k] + drift) + left(here[k] - drift))
                    density_now[1 - i % 2][h, k] = keep * here[k] + share * around

        for q in range(K):
            if q < K - LEAST:
                pl.when(q >= K - most)(lambda q=q: value_step(q))
            else:
                value_step(q)
        for h in range(GROUP):
            put_planes(out_value, (own[h],), value_at, slopes_of(K, h)[0])
        for i in range(K):
            if i >= LEAST:
                pl.when(i < most)(lambda i=i: density_step(i))
            else:
                density_step(i)
        for parity in range(2):

            @pl.when(most % 2 == parity)
            def _(parity=parity):
                for h in range(GROUP):
                    put_planes(out_density, (own[h],), density_at, [density_now[parity][h, k] for k in range(density_n)])

        return carry

    lax.fori_loop(0, SLICES // GROUP, group, 0)


def main_kernel(order, steps, core, own, low, high, far, message, field, factors, reliefs, cost, m0, u0, m1, u1, fm, fu, across, along, sources, va, vb, da, db):
    for part in range(4):

        @pl.when(core[0] == 0)
        def _(part=part):
            field[part, 6:16] = far[part, 6:16]
            field[part, 16:40] = low[part]
            field[part, 40:64] = own[part]
            field[part, 64:86] = high[part, 0:22]

        @pl.when(core[0] != 0)
        def _(part=part):
            field[part, 6:28] = low[part, 2:24]
            field[part, 28:52] = own[part]
            field[part, 52:76] = high[part]
            field[part, 76:86] = far[part, 0:10]

    rate, running = field[3], field[2]
    quotient = running / rate
    for kind in range(KINDS):
        factor = jnp.exp(rate * (-time_step * (LEAST + kind)))
        factors[kind] = factor
        reliefs[kind] = (1.0 - factor) * quotient * (1.0 / SCALE)
    cost[...] = running * (0.5 / SCALE)

    def opening(j, now):
        density, value = now
        back = SLICES - 1 - j
        m0[j] = density
        u0[back] = value
        kind = steps[back] - LEAST
        return factors[steps[j] - LEAST] * density, factors[kind] * value + reliefs[kind]

    lax.fori_loop(0, SLICES, opening, (field[0], field[1] * (1.0 / SCALE)))

    fine_groups(order, steps, u0, m0, planes_of(cost, (), 6, 10), sources, across, along, (va, vb), (da, db), fu, fm, ((6, 10), (14, 8)))

    inner = pl.ds(16, FRAME2)

    def first_sweep(j, now):
        density, value = now
        back = SLICES - 1 - j
        m1[j] = density
        u1[back] = value
        density = factors[steps[j] - LEAST, inner] * (density - m0[j, inner]) + fm[j, inner]
        value = factors[steps[back] - LEAST, inner] * (value - u0[back, inner]) + fu[back, inner]
        return density, value

    lax.fori_loop(0, SLICES, first_sweep, (field[0, inner], field[1, inner] * (1.0 / SCALE)))

    fine_groups(order, steps, u1, m1, planes_of(cost, (), 22, 6), sources, across, along, (va, vb), (da, db), fu, fm, ((6, 6), (16, 4)))

    tile, wide = pl.ds(24, 16), pl.ds(40, 16)
    lane = lax.broadcasted_iota(jnp.int32, (8, LANES), 1)
    for_density, first_rows = lane < 64, (lane % 64) < 32

    def second_sweep(j, now):
        density, value = now
        back = SLICES - 1 - j
        u0[back, 0:16] = value
        m0[j, 0:16] = density
        density = factors[steps[j] - LEAST, wide] * (density - m1[j, tile]) + fm[j, tile]
        value = factors[steps[back] - LEAST, wide] * (value - u1[back, tile]) + fu[back, tile]
        return density, value

    lax.fori_loop(0, SLICES, second_sweep, (field[0, wide], field[1, wide] * (1.0 / SCALE)))

    def moved(plane, lane_now):
        return pltpu.roll(plane, (lane_now - COL_AT) % LANES, 1)

    def packed(j, carry):
        density = jnp.where(first_rows, moved(m0[j, 0:8], 0), moved(m0[j, 8:16], 32))
        value = SCALE * jnp.where(first_rows, moved(u0[j, 0:8], 64), moved(u0[j, 8:16], 96))
        message[j] = jnp.where(for_density, density, value)
        return carry

    lax.fori_loop(0, SLICES, packed, 0)


def window_kernel(place, *refs):
    blocks, (near, far) = refs[:8], refs[8:]
    shift, first = place[2], place[3]
    lane = lax.broadcasted_iota(jnp.int32, (ROWS, LANES), 1)
    for part in range(4):
        a = pltpu.roll(blocks[2 * part][...], shift, 1)
        b = pltpu.roll(blocks[2 * part + 1][...], shift, 1)
        window = jnp.where(lane < shift, a, b)
        near[part] = window

        @pl.when(first == 0)
        def _(window=window, part=part):
            far[part] = window[8:24]

        @pl.when(first != 0)
        def _(window=window, part=part):
            far[part] = window[0:16]


def gather_kernel(received, density, value):
    lane = lax.broadcasted_iota(jnp.int32, (8, LANES), 1)
    for column in range(4):
        for half in range(2):
            for out, base in ((density, 0), (value, 64)):
                for rows, block, begin in ((8, base, 0), (4, base + 32, 8)):
                    whole = None
                    for x in range(4):
                        source = received[column * 8 + x * 2 + half]
                        piece = pltpu.roll(source, (32 * x - block) % LANES, 1)
                        whole = piece if whole is None else jnp.where(lane >= 32 * x, piece, whole)
                    at = TILE_ROWS * half + begin
                    out[0, at : at + rows, LANES * column : LANES * (column + 1)] = whole[0:rows]


def vmem():
    return pl.BlockSpec(memory_space=pltpu.VMEM)


def smem():
    return pl.BlockSpec(memory_space=pltpu.SMEM)


def f32(*shape):
    return jax.ShapeDtypeStruct(shape, jnp.float32)


def windows(place, arrays):
    specs, operands = [], []
    for array in arrays:
        for which in range(2):
            specs.append(pl.BlockSpec((ROWS, LANES), lambda i, place, which=which: (0, place[which])))
            operands.append(array)
    return pl.pallas_call(
        window_kernel,
        out_shape=[f32(4, ROWS, LANES), f32(4, 16, LANES)],
        grid_spec=pltpu.PrefetchScalarGridSpec(
            num_scalar_prefetch=1,
            grid=(1,),
            in_specs=specs,
            out_specs=[
                pl.BlockSpec((4, ROWS, LANES), lambda i, place: (0, 0, 0)),
                pl.BlockSpec((4, 16, LANES), lambda i, place: (0, 0, 0)),
            ],
        ),
        name="windows",
    )(place, *operands)


def both_iterations(order, steps, core, own, low, high, far):
    scratch = [
        (4, FRAME1, LANES),
        (KINDS, FRAME1, LANES),
        (KINDS, FRAME1, LANES),
        (FRAME1, LANES),
        (SLICES, FRAME1, LANES),
        (SLICES, FRAME1, LANES),
        (SLICES, FRAME2, LANES),
        (SLICES, FRAME2, LANES),
        (SLICES, FRAME1, LANES),
        (SLICES, FRAME1, LANES),
        (GROUP, K + 1, FRAME1, LANES),
        (GROUP, K + 1, FRAME1, LANES),
        (GROUP, 10, 8, LANES),
        (GROUP, 10, 8, LANES),
        (GROUP, 10, 8, LANES),
        (GROUP, 10, 8, LANES),
        (GROUP, 10, 8, LANES),
    ]
    return pl.pallas_call(
        main_kernel,
        out_shape=f32(SLICES, 8, LANES),
        in_specs=[smem(), smem(), smem(), vmem(), vmem(), vmem(), vmem()],
        out_specs=vmem(),
        scratch_shapes=[pltpu.VMEM(shape, jnp.float32) for shape in scratch],
        compiler_params=pltpu.CompilerParams(vmem_limit_bytes=32 * 2**20),
        name="both_iterations",
    )(order, steps, core, own, low, high, far)


def gathered(received):
    return pl.pallas_call(
        gather_kernel,
        out_shape=[f32(1, ROWS, 512), f32(1, ROWS, 512)],
        in_specs=[vmem()],
        out_specs=[vmem(), vmem()],
        name="gathered",
    )(received)


def from_offset(array, offset):
    count = 16
    return lax.ppermute(array, SPACE, [((i + offset) % count, i) for i in range(count)])


def on_device(initial_density, terminal_cost, running_cost, discount_rate, slice_steps):
    core = lax.axis_index("c")
    column = lax.axis_index("zh") * 4 + lax.axis_index("x")
    begin = (column * TILE_COLS - COL_AT) % 512
    first_block = begin // LANES
    shift = (LANES - begin % LANES) % LANES
    whole = (shift == 0).astype(jnp.int32)
    place = jnp.stack([first_block, (first_block + 1 - whole) % 4, shift, core]).astype(jnp.int32)
    own, edge = windows(place, (initial_density, terminal_cost, running_cost, discount_rate))
    low = from_offset(own, -1)
    high = from_offset(own, 1)
    hops = []
    for space in range(16):
        for c in range(2):
            source = (space - 2) % 16 if c == 0 else (space + 2) % 16
            hops.append((c * 16 + source, c * 16 + space))
    far = lax.ppermute(edge, ("c", *SPACE), hops)
    numbers = jnp.arange(SLICES, dtype=jnp.int32)
    ahead = (slice_steps[None, :] < slice_steps[:, None]) | ((slice_steps[None, :] == slice_steps[:, None]) & (numbers[None, :] < numbers[:, None]))
    rank = jnp.sum(ahead.astype(jnp.int32), axis=1)
    order = jnp.sum(jnp.where(rank[None, :] == numbers[:, None], numbers[None, :], 0), axis=1)
    message = both_iterations(order, slice_steps, core[None].astype(jnp.int32), own, low, high, far)
    received = lax.all_to_all(message, TM, 0, 0, tiled=True)
    return tuple(gathered(received))


def solution(mesh):
    finer = Mesh(mesh.devices.reshape(4, 4, 2, 8, 2), ("zh", "x", "c", "y", "zl"))
    placed = (P(SPACE, None), P(SPACE, None), P(SPACE, None), P(SPACE, None), P())
    return jax.shard_map(
        on_device,
        mesh=finer,
        in_specs=placed,
        out_specs=(P(TM, SPACE, None), P(TM, SPACE, None)),
        check_vma=False,
    )
```

```python
import jax
import jax.numpy as jnp
from jax import lax
from jax.experimental import pallas as pl
from jax.experimental.pallas import tpu as pltpu
from jax.sharding import Mesh
from jax.sharding import PartitionSpec as P


K = 8
SLICES = 32
LEAST = 4
KINDS = K - LEAST + 1
GROUP = 8
TM = ("zh", "x", "c")
SPACE = ("y", "zl")

time_step = 0.05
diffusion = 2.0
coupling = 0.1

ROWS = 24
TILE_ROWS = 6
TILE_COLS = 64
LANES = 128
COL_AT = 32
FRAME1 = 80
FRAME2 = 48
TOP = 7
PARTS = 5
EDGED = (1, 2, 3)
SCALE = 16.0


def planes_of(ref, at, start, count):
    return [ref[(*at, pl.ds(start + k, 8, stride=count), slice(None))] for k in range(count)]


def put_planes(ref, at, start, planes):
    count = len(planes)
    for k, plane in enumerate(planes):
        ref[(*at, pl.ds(start + k, 8, stride=count), slice(None))] = plane


def row_above(planes):
    return [pltpu.roll(planes[-1], 1, 0), *planes[:-1]]


def row_below(planes):
    return [*planes[1:], pltpu.roll(planes[0], 7, 0)]


def left(plane):
    return pltpu.roll(plane, 1, 1)


def right(plane):
    return pltpu.roll(plane, LANES - 1, 1)


def lanes_of(shape):
    return lax.broadcasted_iota(jnp.int32, shape, len(shape) - 1)


def slope_planes(planes, beside=None):
    up, down = row_above(planes), row_below(planes)
    slopes, sums = [], []
    for k, plane in enumerate(planes):
        west, east = left(plane), right(plane)
        if beside is not None:
            lane = lanes_of(plane.shape)
            west, east = jnp.where(lane == 0, beside[k], west), jnp.where(lane == LANES - 1, beside[k], east)
        slopes.append((down[k] - up[k], east - west))
        sums.append((up[k] + down[k]) + (west + east))
    return slopes, sums


def fine_groups(table, values, beside, densities, cost, sources, across, along, value_now, density_now, out_value, out_density, spots):
    (value_at, value_n), (density_at, density_n) = spots
    keep_all, share_all = 1.0 - 4.0 * time_step * diffusion, time_step * diffusion

    def group(number, carry):
        own = [table[GROUP * number + h] for h in range(GROUP)]
        trips = [table[SLICES + j] for j in own]
        most = trips[-1]
        for h in range(GROUP):
            start = planes_of(values, (own[h],), value_at, value_n)
            held = planes_of(densities, (own[h],), value_at, value_n)
            for k in range(value_n):
                value_now[0][h, k] = value_now[1][h, k] = start[k]
                sources[h, k] = cost[k] + (0.5 / SCALE * coupling) * held[k]
            for k, plane in enumerate(planes_of(densities, (own[h],), density_at, density_n)):
                density_now[0][h, k] = plane

        def slopes_of(q, h):
            now = [value_now[q % 2][h, k] for k in range(value_n)]
            edges = planes_of(beside, (own[h],), value_at, value_n) if q == 0 and beside is not None else None
            slopes, sums = slope_planes(now, edges)
            put_planes(across, (h, q), value_at, [a for a, _ in slopes])
            put_planes(along, (h, q), value_at, [b for _, b in slopes])
            return now, slopes, sums

        def value_step(q):
            for h in range(GROUP):
                keep, share = keep_all, share_all
                if q < K - LEAST:
                    active = q >= K - trips[h]
                    keep, share = jnp.where(active, keep, 1.0), jnp.where(active, share, 0.0)
                now, slopes, sums = slopes_of(q, h)
                for k in range(value_n):
                    a, b = slopes[k]
                    value_now[1 - q % 2][h, k] = keep * now[k] + share * (sums[k] + (sources[h, k] - (a * a + b * b)))

        def density_step(i):
            for h in range(GROUP):
                keep, share = keep_all, share_all
                if i >= LEAST:
                    active = i < trips[h]
                    keep, share = jnp.where(active, keep, 1.0), jnp.where(active, share, 0.0)
                a = planes_of(across, (h, K - i), density_at, density_n)
                b = planes_of(along, (h, K - i), density_at, density_n)
                here = [density_now[i % 2][h, k] for k in range(density_n)]
                twice = [plane + plane for plane in here]
                flux = [twice[k] * a[k] for k in range(density_n)]
                below = row_below([here[k] + flux[k] for k in range(density_n)])
                above = row_above([here[k] - flux[k] for k in range(density_n)])
                for k in range(density_n):
                    drift = twice[k] * b[k]
                    around = (below[k] + above[k]) + (right(here[k] + drift) + left(here[k] - drift))
                    density_now[1 - i % 2][h, k] = keep * here[k] + share * around

        for q in range(K):
            if q < K - LEAST:
                pl.when(q >= K - most)(lambda q=q: value_step(q))
            else:
                value_step(q)
        for h in range(GROUP):
            put_planes(out_value, (own[h],), value_at, slopes_of(K, h)[0])
        for i in range(K):
            if i >= LEAST:
                pl.when(i < most)(lambda i=i: density_step(i))
            else:
                density_step(i)
        for parity in range(2):

            @pl.when(most % 2 == parity)
            def _(parity=parity):
                for h in range(GROUP):
                    put_planes(out_density, (own[h],), density_at, [density_now[parity][h, k] for k in range(density_n)])

        return carry

    lax.fori_loop(0, SLICES // GROUP, group, 0)


def main_kernel(table, own, near, far, message, field, factors, reliefs, cost, m0, u0, e0, m1, u1, fm, fu, across, along, sources, va, vb, da, db):
    band, half = table[2 * SLICES], table[2 * SLICES + 1]
    for position in range(4):

        @pl.when(band == position)
        def _(position=position):
            pieces = [(near, (0,), ROWS, -24), (own, (), ROWS, 0), (near, (1,), ROWS, 24), (far, (), 16, -40 if position < 2 else 48)]
            for ref, at, rows, first in pieces:
                begin = first - TILE_ROWS * position + 40
                low, high = max(begin, TOP), min(begin + rows, FRAME1 - 1)
                for part in range(PARTS):
                    field[part, low:high] = ref[(*at, part, slice(low - begin, high - begin))]

    packed_edges = field[4]
    lane = lanes_of((FRAME1, LANES))
    edges = {}
    for place, part in enumerate(EDGED):
        edges[part] = jnp.where(lane < 64, pltpu.roll(packed_edges, (LANES - place) % LANES, 1), pltpu.roll(packed_edges, place, 1)) if place else packed_edges
    for begin, rate, running in ((0, field[3], field[2]), (KINDS, edges[3], edges[2])):
        quotient = running / rate
        for kind in range(KINDS):
            factor = jnp.exp(rate * (-time_step * (LEAST + kind)))
            factors[begin + kind] = factor
            reliefs[begin + kind] = (1.0 - factor) * quotient * (1.0 / SCALE)
    cost[...] = field[2] * (0.5 / SCALE)

    def opening(j, now):
        density, value, edge = now
        back = SLICES - 1 - j
        m0[j] = density
        u0[back] = value
        e0[back] = edge
        kind = table[SLICES + back] - LEAST
        density = factors[table[SLICES + j] - LEAST] * density
        value = factors[kind] * value + reliefs[kind]
        edge = factors[KINDS + kind] * edge + reliefs[KINDS + kind]
        return density, value, edge

    lax.fori_loop(0, SLICES, opening, (field[0], field[1] * (1.0 / SCALE), edges[1] * (1.0 / SCALE)))

    fine_groups(table, u0, e0, m0, planes_of(cost, (), 7, 9), sources, across, along, (va, vb), (da, db), fu, fm, ((7, 9), (15, 7)))

    inner = pl.ds(16, FRAME2)

    def first_sweep(j, now):
        density, value = now
        back = SLICES - 1 - j
        m1[j] = density
        u1[back] = value
        density = factors[table[SLICES + j] - LEAST, inner] * (density - m0[j, inner]) + fm[j, inner]
        value = factors[table[SLICES + back] - LEAST, inner] * (value - u0[back, inner]) + fu[back, inner]
        return density, value

    lax.fori_loop(0, SLICES, first_sweep, (field[0, inner], field[1, inner] * (1.0 / SCALE)))

    fine_groups(table, u1, None, m1, planes_of(cost, (), 23, 5), sources, across, along, (va, vb), (da, db), fu, fm, ((7, 5), (15, 3)))

    tile, wide = pl.ds(24, 8), pl.ds(40, 8)

    def second_sweep(j, now):
        density, value = now
        back = SLICES - 1 - j
        u0[back, 0:8] = value
        m0[j, 0:8] = density
        density = factors[table[SLICES + j] - LEAST, wide] * (density - m1[j, tile]) + fm[j, tile]
        value = factors[table[SLICES + back] - LEAST, wide] * (value - u1[back, tile]) + fu[back, tile]
        return density, value

    lax.fori_loop(0, SLICES, second_sweep, (field[0, wide], field[1, wide] * (1.0 / SCALE)))

    first_half = lanes_of((8, LANES)) < 64
    for j in range(SLICES):
        density, value = m0[j, 0:8], SCALE * u0[j, 0:8]
        ahead, behind = jnp.where(half == 0, density, value), jnp.where(half == 0, value, density)
        message[j] = jnp.where(first_half, pltpu.roll(ahead, LANES - COL_AT, 1), pltpu.roll(behind, COL_AT, 1))


def place_of():
    zh, x, c = (lax.axis_index(axis) for axis in TM)
    return 2 * c + x % 2, 2 * zh + x // 2, x // 2, c


def window_kernel(*refs):
    arrays, (near, far), (blocks, arrived) = refs[:4], refs[4:6], refs[6:]
    _, column, _, core = place_of()
    begin = (column * TILE_COLS + 512 - COL_AT) % 512
    first, shift = begin // LANES, LANES - begin % LANES
    copies = []
    for part, array in enumerate(arrays):
        for which in range(2):
            at = pl.multiple_of(((first + which) % 4) * LANES, LANES)
            copies.append(pltpu.make_async_copy(array.at[:, pl.ds(at, LANES)], blocks.at[part, which], arrived.at[part, which]))
    for copy in copies:
        copy.start()
    for copy in copies:
        copy.wait()
    lane = lanes_of((ROWS, LANES))
    beside = jnp.zeros((ROWS, LANES), jnp.float32)
    for part in range(PARTS):
        if part < 4:
            a, b = blocks[part, 0], blocks[part, 1]
            window = jnp.where(lane < shift, pltpu.roll(a, shift, 1), pltpu.roll(b, shift, 1))
        else:
            window = beside
        near[part] = window

        @pl.when(core == 0)
        def _(window=window, part=part):
            far[part] = window[8:24]

        @pl.when(core != 0)
        def _(window=window, part=part):
            far[part] = window[0:16]

        if part in EDGED:
            place = EDGED.index(part)
            beside = jnp.where(lane == place, pltpu.roll(a, shift + 1 + place, 1), beside)
            beside = jnp.where(lane == LANES - 1 - place, pltpu.roll(b, shift - 1 - place, 1), beside)


def gather_kernel(received, density, value):
    first_half = lanes_of((8, LANES)) < 64
    for zh in range(4):
        for band in range(4):
            at = [zh * 8 + (2 * half + band % 2) * 2 + band // 2 for half in range(2)]
            a, b = received[at[0]], received[at[1]]
            rows, lanes = slice(TILE_ROWS * band, TILE_ROWS * (band + 1)), slice(LANES * zh, LANES * (zh + 1))
            density[0, rows, lanes] = jnp.where(first_half, a, b)[0:TILE_ROWS]
            value[0, rows, lanes] = pltpu.roll(jnp.where(first_half, b, a), 64, 1)[0:TILE_ROWS]


def vmem():
    return pl.BlockSpec(memory_space=pltpu.VMEM)


def smem():
    return pl.BlockSpec(memory_space=pltpu.SMEM)


def f32(*shape):
    return jax.ShapeDtypeStruct(shape, jnp.float32)


def windows(*arrays):
    return pl.pallas_call(
        window_kernel,
        out_shape=[f32(PARTS, ROWS, LANES), f32(PARTS, 16, LANES)],
        in_specs=[pl.BlockSpec(memory_space=pl.ANY)] * 4,
        out_specs=[vmem(), vmem()],
        scratch_shapes=[pltpu.VMEM((4, 2, ROWS, LANES), jnp.float32), pltpu.SemaphoreType.DMA((4, 2))],
        name="windows",
    )(*arrays)


def both_iterations(table, own, near, far):
    scratch = [
        (PARTS, FRAME1, LANES),
        (2 * KINDS, FRAME1, LANES),
        (2 * KINDS, FRAME1, LANES),
        (FRAME1, LANES),
        (SLICES, FRAME1, LANES),
        (SLICES, FRAME1, LANES),
        (SLICES, FRAME1, LANES),
        (SLICES, FRAME2, LANES),
        (SLICES, FRAME2, LANES),
        (SLICES, FRAME1, LANES),
        (SLICES, FRAME1, LANES),
        (GROUP, K + 1, FRAME1, LANES),
        (GROUP, K + 1, FRAME1, LANES),
        (GROUP, 9, 8, LANES),
        (GROUP, 9, 8, LANES),
        (GROUP, 9, 8, LANES),
        (GROUP, 9, 8, LANES),
        (GROUP, 9, 8, LANES),
    ]
    return pl.pallas_call(
        main_kernel,
        out_shape=f32(SLICES, 8, LANES),
        in_specs=[smem(), vmem(), vmem(), vmem()],
        out_specs=vmem(),
        scratch_shapes=[pltpu.VMEM(shape, jnp.float32) for shape in scratch],
        compiler_params=pltpu.CompilerParams(vmem_limit_bytes=32 * 2**20),
        name="both_iterations",
    )(table, own, near, far)


def gathered(received):
    return pl.pallas_call(
        gather_kernel,
        out_shape=[f32(1, ROWS, 512), f32(1, ROWS, 512)],
        in_specs=[vmem()],
        out_specs=[vmem(), vmem()],
        name="gathered",
    )(received)


def toward_own_side(array, distance):
    hops = []
    for c in range(2):
        for space in range(16):
            source = (space + (distance if c else -distance)) % 16
            hops.append((c * 16 + source, c * 16 + space))
    return lax.ppermute(array, ("c", *SPACE), hops)


def on_device(initial_density, terminal_cost, running_cost, discount_rate, slice_steps):
    own, edge = windows(initial_density, terminal_cost, running_cost, discount_rate)
    beside = toward_own_side(own, 1)
    far = toward_own_side(edge, 2)
    near = lax.all_gather(beside, "c")
    band, _, half, _ = place_of()
    numbers = jnp.arange(SLICES, dtype=jnp.int32)
    ahead = (slice_steps[None, :] < slice_steps[:, None]) | ((slice_steps[None, :] == slice_steps[:, None]) & (numbers[None, :] < numbers[:, None]))
    rank = jnp.sum(ahead.astype(jnp.int32), axis=1)
    order = jnp.sum(jnp.where(rank[None, :] == numbers[:, None], numbers[None, :], 0), axis=1)
    table = jnp.concatenate([order, slice_steps, jnp.stack([band, half]).astype(jnp.int32)])
    message = both_iterations(table, own, near, far)
    received = lax.all_to_all(message, TM, 0, 0, tiled=True)
    return tuple(gathered(received))


def solution(mesh):
    finer = Mesh(mesh.devices.reshape(4, 4, 2, 8, 2), ("zh", "x", "c", "y", "zl"))
    placed = (P(SPACE, None), P(SPACE, None), P(SPACE, None), P(SPACE, None), P())
    return jax.shard_map(
        on_device,
        mesh=finer,
        in_specs=placed,
        out_specs=(P(TM, SPACE, None), P(TM, SPACE, None)),
        check_vma=False,
    )
```

```python
import jax
import jax.numpy as jnp
from jax import lax
from jax.experimental import pallas as pl
from jax.experimental.pallas import tpu as pltpu
from jax.sharding import Mesh
from jax.sharding import PartitionSpec as P


K = 8
SLICES = 32
LEAST = 4
KINDS = K - LEAST + 1
GROUP = 8
TM = ("zh", "x", "c")
SPACE = ("y", "zl")

time_step = 0.05
diffusion = 2.0
coupling = 0.1

ROWS = 24
TILE_ROWS = 6
TILE_COLS = 64
LANES = 128
COL_AT = 32
FRAME1 = 80
FRAME2 = 48
TOP = 7
PARTS = 5
EDGED = (1, 2, 3)
SCALE = 16.0


def planes_of(ref, at, start, count):
    return [ref[(*at, pl.ds(start + k, 8, stride=count), slice(None))] for k in range(count)]


def put_planes(ref, at, start, planes):
    count = len(planes)
    for k, plane in enumerate(planes):
        ref[(*at, pl.ds(start + k, 8, stride=count), slice(None))] = plane


def row_above(planes):
    return [pltpu.roll(planes[-1], 1, 0), *planes[:-1]]


def row_below(planes):
    return [*planes[1:], pltpu.roll(planes[0], 7, 0)]


def left(plane):
    return pltpu.roll(plane, 1, 1)


def right(plane):
    return pltpu.roll(plane, LANES - 1, 1)


def lanes_of(shape):
    return lax.broadcasted_iota(jnp.int32, shape, len(shape) - 1)


def slope_planes(planes, beside=None):
    up, down = row_above(planes), row_below(planes)
    slopes, sums = [], []
    for k, plane in enumerate(planes):
        west, east = left(plane), right(plane)
        if beside is not None:
            lane = lanes_of(plane.shape)
            west, east = jnp.where(lane == 0, beside[k], west), jnp.where(lane == LANES - 1, beside[k], east)
        slopes.append((down[k] - up[k], east - west))
        sums.append((up[k] + down[k]) + (west + east))
    return slopes, sums


def fine_groups(table, values, beside, densities, cost, sources, across, along, value_now, density_now, out_value, out_density, spots):
    (value_at, value_n), (density_at, density_n) = spots
    keep_all, share_all = 1.0 - 4.0 * time_step * diffusion, time_step * diffusion

    def group(number, carry):
        own = [table[GROUP * number + h] for h in range(GROUP)]
        trips = [table[SLICES + j] for j in own]
        most = trips[-1]
        for h in range(GROUP):
            start = planes_of(values, (own[h],), value_at, value_n)
            held = planes_of(densities, (own[h],), value_at, value_n)
            for k in range(value_n):
                value_now[0][h, k] = value_now[1][h, k] = start[k]
                sources[h, k] = cost[k] + (0.5 / SCALE * coupling) * held[k]
            for k, plane in enumerate(planes_of(densities, (own[h],), density_at, density_n)):
                density_now[0][h, k] = plane

        def slopes_of(q, h):
            now = [value_now[q % 2][h, k] for k in range(value_n)]
            edges = planes_of(beside, (own[h],), value_at, value_n) if q == 0 and beside is not None else None
            slopes, sums = slope_planes(now, edges)
            put_planes(across, (h, q), value_at, [a for a, _ in slopes])
            put_planes(along, (h, q), value_at, [b for _, b in slopes])
            return now, slopes, sums

        def value_step(q):
            for h in range(GROUP):
                keep, share = keep_all, share_all
                if q < K - LEAST:
                    active = q >= K - trips[h]
                    keep, share = jnp.where(active, keep, 1.0), jnp.where(active, share, 0.0)
                now, slopes, sums = slopes_of(q, h)
                for k in range(value_n):
                    a, b = slopes[k]
                    value_now[1 - q % 2][h, k] = keep * now[k] + share * (sums[k] + (sources[h, k] - (a * a + b * b)))

        def density_step(i):
            for h in range(GROUP):
                keep, share = keep_all, share_all
                if i >= LEAST:
                    active = i < trips[h]
                    keep, share = jnp.where(active, keep, 1.0), jnp.where(active, share, 0.0)
                a = planes_of(across, (h, K - i), density_at, density_n)
                b = planes_of(along, (h, K - i), density_at, density_n)
                here = [density_now[i % 2][h, k] for k in range(density_n)]
                twice = [plane + plane for plane in here]
                flux = [twice[k] * a[k] for k in range(density_n)]
                below = row_below([here[k] + flux[k] for k in range(density_n)])
                above = row_above([here[k] - flux[k] for k in range(density_n)])
                for k in range(density_n):
                    drift = twice[k] * b[k]
                    around = (below[k] + above[k]) + (right(here[k] + drift) + left(here[k] - drift))
                    density_now[1 - i % 2][h, k] = keep * here[k] + share * around

        for q in range(K):
            if q < K - LEAST:
                pl.when(q >= K - most)(lambda q=q: value_step(q))
            else:
                value_step(q)
        for h in range(GROUP):
            put_planes(out_value, (own[h],), value_at, slopes_of(K, h)[0])
        for i in range(K):
            if i >= LEAST:
                pl.when(i < most)(lambda i=i: density_step(i))
            else:
                density_step(i)
        for parity in range(2):

            @pl.when(most % 2 == parity)
            def _(parity=parity):
                for h in range(GROUP):
                    put_planes(out_density, (own[h],), density_at, [density_now[parity][h, k] for k in range(density_n)])

        return carry

    lax.fori_loop(0, SLICES // GROUP, group, 0)


def main_kernel(table, own, near, far, message, field, factors, reliefs, cost, m0, u0, e0, m1, u1, fm, fu, across, along, sources, va, vb, da, db):
    band, half = table[2 * SLICES], table[2 * SLICES + 1]
    for position in range(4):

        @pl.when(band == position)
        def _(position=position):
            pieces = [(near, (0,), ROWS, -24), (own, (), ROWS, 0), (near, (1,), ROWS, 24), (far, (), 16, -40 if position < 2 else 48)]
            for ref, at, rows, first in pieces:
                begin = first - TILE_ROWS * position + 40
                low, high = max(begin, TOP), min(begin + rows, FRAME1 - 1)
                for part in range(PARTS):
                    field[part, low:high] = ref[(*at, part, slice(low - begin, high - begin))]

    packed_edges = field[4]
    lane = lanes_of((FRAME1, LANES))
    edges = {}
    for place, part in enumerate(EDGED):
        edges[part] = jnp.where(lane < 64, pltpu.roll(packed_edges, (LANES - place) % LANES, 1), pltpu.roll(packed_edges, place, 1)) if place else packed_edges
    for begin, rate, running in ((0, field[3], field[2]), (KINDS, edges[3], edges[2])):
        quotient = running / rate
        for kind in range(KINDS):
            factor = jnp.exp(rate * (-time_step * (LEAST + kind)))
            factors[begin + kind] = factor
            reliefs[begin + kind] = (1.0 - factor) * quotient * (1.0 / SCALE)
    cost[...] = field[2] * (0.5 / SCALE)

    def opening(j, now):
        density, value, edge = now
        back = SLICES - 1 - j
        m0[j] = density
        u0[back] = value
        e0[back] = edge
        kind = table[SLICES + back] - LEAST
        density = factors[table[SLICES + j] - LEAST] * density
        value = factors[kind] * value + reliefs[kind]
        edge = factors[KINDS + kind] * edge + reliefs[KINDS + kind]
        return density, value, edge

    lax.fori_loop(0, SLICES, opening, (field[0], field[1] * (1.0 / SCALE), edges[1] * (1.0 / SCALE)), unroll=2)

    fine_groups(table, u0, e0, m0, planes_of(cost, (), 7, 9), sources, across, along, (va, vb), (da, db), fu, fm, ((7, 9), (15, 7)))

    inner = pl.ds(16, FRAME2)

    def first_sweep(j, now):
        density, value = now
        back = SLICES - 1 - j
        m1[j] = density
        u1[back] = value
        density = factors[table[SLICES + j] - LEAST, inner] * (density - m0[j, inner]) + fm[j, inner]
        value = factors[table[SLICES + back] - LEAST, inner] * (value - u0[back, inner]) + fu[back, inner]
        return density, value

    lax.fori_loop(0, SLICES, first_sweep, (field[0, inner], field[1, inner] * (1.0 / SCALE)), unroll=4)

    fine_groups(table, u1, None, m1, planes_of(cost, (), 23, 5), sources, across, along, (va, vb), (da, db), fu, fm, ((7, 5), (15, 3)))

    tile, wide = pl.ds(24, 8), pl.ds(40, 8)

    def second_sweep(j, now):
        density, value = now
        back = SLICES - 1 - j
        u0[back, 0:8] = value
        m0[j, 0:8] = density
        density = factors[table[SLICES + j] - LEAST, wide] * (density - m1[j, tile]) + fm[j, tile]
        value = factors[table[SLICES + back] - LEAST, wide] * (value - u1[back, tile]) + fu[back, tile]
        return density, value

    lax.fori_loop(0, SLICES, second_sweep, (field[0, wide], field[1, wide] * (1.0 / SCALE)), unroll=8)

    first_half = lanes_of((8, LANES)) < 64
    for j in range(SLICES):
        density, value = m0[j, 0:8], SCALE * u0[j, 0:8]
        ahead, behind = jnp.where(half == 0, density, value), jnp.where(half == 0, value, density)
        message[j] = jnp.where(first_half, pltpu.roll(ahead, LANES - COL_AT, 1), pltpu.roll(behind, COL_AT, 1))


def place_of():
    zh, x, c = (lax.axis_index(axis) for axis in TM)
    return 2 * c + x % 2, 2 * zh + x // 2, x // 2, c


def window_kernel(*refs):
    arrays, (near, far), (blocks, arrived) = refs[:4], refs[4:6], refs[6:]
    _, column, _, core = place_of()
    begin = (column * TILE_COLS + 512 - COL_AT) % 512
    first, shift = begin // LANES, LANES - begin % LANES
    copies = []
    for part, array in enumerate(arrays):
        for which in range(2):
            at = pl.multiple_of(((first + which) % 4) * LANES, LANES)
            copies.append(pltpu.make_async_copy(array.at[:, pl.ds(at, LANES)], blocks.at[part, which], arrived.at[part, which]))
    for copy in copies:
        copy.start()
    for copy in copies:
        copy.wait()
    lane = lanes_of((ROWS, LANES))
    beside = jnp.zeros((ROWS, LANES), jnp.float32)
    for part in range(PARTS):
        if part < 4:
            a, b = blocks[part, 0], blocks[part, 1]
            window = jnp.where(lane < shift, pltpu.roll(a, shift, 1), pltpu.roll(b, shift, 1))
        else:
            window = beside
        near[part] = window

        @pl.when(core == 0)
        def _(window=window, part=part):
            far[part] = window[8:24]

        @pl.when(core != 0)
        def _(window=window, part=part):
            far[part] = window[0:16]

        if part in EDGED:
            place = EDGED.index(part)
            beside = jnp.where(lane == place, pltpu.roll(a, shift + 1 + place, 1), beside)
            beside = jnp.where(lane == LANES - 1 - place, pltpu.roll(b, shift - 1 - place, 1), beside)


def gather_kernel(received, density, value):
    first_half = lanes_of((8, LANES)) < 64
    for zh in range(4):
        for band in range(4):
            at = [zh * 8 + (2 * half + band % 2) * 2 + band // 2 for half in range(2)]
            a, b = received[at[0]], received[at[1]]
            rows, lanes = slice(TILE_ROWS * band, TILE_ROWS * (band + 1)), slice(LANES * zh, LANES * (zh + 1))
            density[0, rows, lanes] = jnp.where(first_half, a, b)[0:TILE_ROWS]
            value[0, rows, lanes] = pltpu.roll(jnp.where(first_half, b, a), 64, 1)[0:TILE_ROWS]


def vmem():
    return pl.BlockSpec(memory_space=pltpu.VMEM)


def smem():
    return pl.BlockSpec(memory_space=pltpu.SMEM)


def f32(*shape):
    return jax.ShapeDtypeStruct(shape, jnp.float32)


def windows(*arrays):
    return pl.pallas_call(
        window_kernel,
        out_shape=[f32(PARTS, ROWS, LANES), f32(PARTS, 16, LANES)],
        in_specs=[pl.BlockSpec(memory_space=pl.ANY)] * 4,
        out_specs=[vmem(), vmem()],
        scratch_shapes=[pltpu.VMEM((4, 2, ROWS, LANES), jnp.float32), pltpu.SemaphoreType.DMA((4, 2))],
        name="windows",
    )(*arrays)


def both_iterations(table, own, near, far):
    scratch = [
        (PARTS, FRAME1, LANES),
        (2 * KINDS, FRAME1, LANES),
        (2 * KINDS, FRAME1, LANES),
        (FRAME1, LANES),
        (SLICES, FRAME1, LANES),
        (SLICES, FRAME1, LANES),
        (SLICES, FRAME1, LANES),
        (SLICES, FRAME2, LANES),
        (SLICES, FRAME2, LANES),
        (SLICES, FRAME1, LANES),
        (SLICES, FRAME1, LANES),
        (GROUP, K + 1, FRAME1, LANES),
        (GROUP, K + 1, FRAME1, LANES),
        (GROUP, 9, 8, LANES),
        (GROUP, 9, 8, LANES),
        (GROUP, 9, 8, LANES),
        (GROUP, 9, 8, LANES),
        (GROUP, 9, 8, LANES),
    ]
    return pl.pallas_call(
        main_kernel,
        out_shape=f32(SLICES, 8, LANES),
        in_specs=[smem(), vmem(), vmem(), vmem()],
        out_specs=vmem(),
        scratch_shapes=[pltpu.VMEM(shape, jnp.float32) for shape in scratch],
        compiler_params=pltpu.CompilerParams(vmem_limit_bytes=32 * 2**20),
        name="both_iterations",
    )(table, own, near, far)


def gathered(received):
    return pl.pallas_call(
        gather_kernel,
        out_shape=[f32(1, ROWS, 512), f32(1, ROWS, 512)],
        in_specs=[vmem()],
        out_specs=[vmem(), vmem()],
        compiler_params=pltpu.CompilerParams(vmem_limit_bytes=2 * 2**20),
        name="gathered",
    )(received)


def toward_own_side(array, distance):
    hops = []
    for c in range(2):
        for space in range(16):
            source = (space + (distance if c else -distance)) % 16
            hops.append((c * 16 + source, c * 16 + space))
    return lax.ppermute(array, ("c", *SPACE), hops)


def on_device(initial_density, terminal_cost, running_cost, discount_rate, slice_steps):
    own, edge = windows(initial_density, terminal_cost, running_cost, discount_rate)
    beside = toward_own_side(own, 1)
    near = lax.all_gather(beside, "c")
    band, _, half, _ = place_of()
    numbers = jnp.arange(SLICES, dtype=jnp.int32)
    ahead = (slice_steps[None, :] < slice_steps[:, None]) | ((slice_steps[None, :] == slice_steps[:, None]) & (numbers[None, :] < numbers[:, None]))
    rank = jnp.sum(ahead.astype(jnp.int32), axis=1)
    order = jnp.sum(jnp.where(rank[None, :] == numbers[:, None], numbers[None, :], 0), axis=1)
    table = jnp.concatenate([order, slice_steps, jnp.stack([band, half]).astype(jnp.int32)])
    edge, table = lax.optimization_barrier((edge, table))
    far = toward_own_side(edge, 2)
    message = both_iterations(table, own, near, far)
    received = lax.all_to_all(message, TM, 0, 0, tiled=True)
    return tuple(gathered(received))


def solution(mesh):
    finer = Mesh(mesh.devices.reshape(4, 4, 2, 8, 2), ("zh", "x", "c", "y", "zl"))
    placed = (P(SPACE, None), P(SPACE, None), P(SPACE, None), P(SPACE, None), P())
    return jax.shard_map(
        on_device,
        mesh=finer,
        in_specs=placed,
        out_specs=(P(TM, SPACE, None), P(TM, SPACE, None)),
        check_vma=False,
    )
```

```python
import jax
import jax.numpy as jnp
from jax import lax
from jax.experimental import pallas as pl
from jax.experimental.pallas import tpu as pltpu
from jax.sharding import Mesh
from jax.sharding import PartitionSpec as P


K = 8
SLICES = 32
LEAST = 4
KINDS = K - LEAST + 1
GROUP1 = 16
GROUP2 = 16
GROUP = max(GROUP1, GROUP2)
PAIRS = GROUP // 2
HALF = 64
TM = ("zh", "x", "c")
SPACE = ("y", "zl")

time_step = 0.05
diffusion = 2.0
coupling = 0.1

ROWS = 24
TILE_ROWS = 6
TILE_COLS = 64
LANES = 128
COL_AT = 32
FRAME1 = 80
FRAME2 = 48
TOP = 7
PARTS = 5
EDGED = (1, 2, 3)
SCALE = 16.0


def planes_of(ref, at, start, count):
    return [ref[(*at, pl.ds(start + k, 8, stride=count), slice(None))] for k in range(count)]


def put_planes(ref, at, start, planes):
    count = len(planes)
    for k, plane in enumerate(planes):
        ref[(*at, pl.ds(start + k, 8, stride=count), slice(None))] = plane


def row_above(planes):
    return [pltpu.roll(planes[-1], 1, 0), *planes[:-1]]


def row_below(planes):
    return [*planes[1:], pltpu.roll(planes[0], 7, 0)]


def left(plane):
    return pltpu.roll(plane, 1, 1)


def right(plane):
    return pltpu.roll(plane, LANES - 1, 1)


def lanes_of(shape):
    return lax.broadcasted_iota(jnp.int32, shape, len(shape) - 1)


def paired(a, b):
    first = lanes_of(a.shape) < HALF
    return jnp.where(first, a, pltpu.roll(b, HALF, 1)), jnp.where(first, pltpu.roll(a, HALF, 1), b)


def pair_planes(many_a, many_b):
    both = [paired(a, b) for a, b in zip(many_a, many_b)]
    return [even for even, _ in both], [odd for _, odd in both]


def slope_planes(even, odd, beside=None):
    result = []
    for parity, planes in enumerate((even, odd)):
        up, down = row_above(planes), row_below(planes)
        slopes, sums = [], []
        for k in range(len(planes)):
            if parity == 0:
                west, east = left(odd[k]), odd[k]
                if beside is not None:
                    west = jnp.where(lanes_of(west.shape) % HALF == 0, beside[0][k], west)
            else:
                west, east = even[k], right(even[k])
                if beside is not None:
                    east = jnp.where(lanes_of(east.shape) % HALF == HALF - 1, beside[1][k], east)
            slopes.append((down[k] - up[k], east - west))
            sums.append((up[k] + down[k]) + (west + east))
        result.append((planes, slopes, sums))
    return result


def fine_groups(size, table, values, beside, densities, cost, sources, across, along, value_now, density_now, out_value, out_density, spots):
    (value_at, value_n), (density_at, density_n) = spots
    keep_all, share_all = 1.0 - 4.0 * time_step * diffusion, time_step * diffusion
    costs = pair_planes(cost, cost)
    first = lanes_of((8, LANES)) < HALF

    def group(number, carry):
        own = [table[size * number + h] for h in range(size)]
        trips = [table[SLICES + j] for j in own]
        most = trips[-1]

        def taken(ref, at, n, h):
            return pair_planes(*[planes_of(ref, (own[2 * h + side],), at, n) for side in range(2)])

        def left_at(ref, at, h, both):
            for side, planes in enumerate(pair_planes(*both)):
                put_planes(ref, (own[2 * h + side],), at, planes)

        def weights(h, test):
            on = [test(trips[2 * h + side]) for side in range(2)]
            keep = jnp.where(first, jnp.where(on[0], keep_all, 1.0), jnp.where(on[1], keep_all, 1.0))
            share = jnp.where(first, jnp.where(on[0], share_all, 0.0), jnp.where(on[1], share_all, 0.0))
            return keep, share

        for h in range(size // 2):
            start, held, density = taken(values, value_at, value_n, h), taken(densities, value_at, value_n, h), taken(densities, density_at, density_n, h)
            for parity in range(2):
                for k in range(value_n):
                    value_now[0][h, parity, k] = value_now[1][h, parity, k] = start[parity][k]
                    sources[h, parity, k] = costs[parity][k] + (0.5 / SCALE * coupling) * held[parity][k]
                for k in range(density_n):
                    density_now[0][h, parity, k] = density[parity][k]

        def slopes_of(q, h):
            now = [[value_now[q % 2][h, parity, k] for k in range(value_n)] for parity in range(2)]
            edges = taken(beside, value_at, value_n, h) if q == 0 and beside is not None else None
            result = slope_planes(*now, edges)
            for parity in range(2):
                put_planes(across, (2 * h + parity, q), value_at, [a for a, _ in result[parity][1]])
                put_planes(along, (2 * h + parity, q), value_at, [b for _, b in result[parity][1]])
            return result

        def value_step(q):
            for h in range(size // 2):
                keep, share = keep_all, share_all
                if q < K - LEAST:
                    keep, share = weights(h, lambda count: q >= K - count)
                for parity, (now, slopes, sums) in enumerate(slopes_of(q, h)):
                    for k in range(value_n):
                        a, b = slopes[k]
                        value_now[1 - q % 2][h, parity, k] = keep * now[k] + share * (sums[k] + (sources[h, parity, k] - (a * a + b * b)))

        def density_step(i):
            for h in range(size // 2):
                keep, share = keep_all, share_all
                if i >= LEAST:
                    keep, share = weights(h, lambda count: i < count)
                here, rows, more, less = [], [], [], []
                for parity in range(2):
                    a = planes_of(across, (2 * h + parity, K - i), density_at, density_n)
                    b = planes_of(along, (2 * h + parity, K - i), density_at, density_n)
                    now = [density_now[i % 2][h, parity, k] for k in range(density_n)]
                    twice = [plane + plane for plane in now]
                    flux = [twice[k] * a[k] for k in range(density_n)]
                    below = row_below([now[k] + flux[k] for k in range(density_n)])
                    above = row_above([now[k] - flux[k] for k in range(density_n)])
                    drift = [twice[k] * b[k] for k in range(density_n)]
                    here.append(now)
                    rows.append([below[k] + above[k] for k in range(density_n)])
                    more.append([now[k] + drift[k] for k in range(density_n)])
                    less.append([now[k] - drift[k] for k in range(density_n)])
                for k in range(density_n):
                    around = (rows[0][k] + more[1][k]) + left(less[1][k]), (rows[1][k] + less[0][k]) + right(more[0][k])
                    for parity in range(2):
                        density_now[1 - i % 2][h, parity, k] = keep * here[parity][k] + share * around[parity]

        for q in range(K):
            if q < K - LEAST:
                pl.when(q >= K - most)(lambda q=q: value_step(q))
            else:
                value_step(q)
        for h in range(size // 2):
            left_at(out_value, value_at, h, [planes for planes, _, _ in slopes_of(K, h)])
        for i in range(K):
            if i >= LEAST:
                pl.when(i < most)(lambda i=i: density_step(i))
            else:
                density_step(i)
        for last in range(2):

            @pl.when(most % 2 == last)
            def _(last=last):
                for h in range(size // 2):
                    left_at(out_density, density_at, h, [[density_now[last][h, parity, k] for k in range(density_n)] for parity in range(2)])

        return carry

    lax.fori_loop(0, SLICES // size, group, 0)


def main_kernel(table, own, near, far, message, field, factors, reliefs, cost, m0, u0, e0, m1, u1, fm, fu, across, along, sources, va, vb, da, db):
    band, half = table[2 * SLICES], table[2 * SLICES + 1]
    for position in range(4):

        @pl.when(band == position)
        def _(position=position):
            pieces = [(near, (0,), ROWS, -24), (own, (), ROWS, 0), (near, (1,), ROWS, 24), (far, (), 16, -40 if position < 2 else 48)]
            for ref, at, rows, first in pieces:
                begin = first - TILE_ROWS * position + 40
                low, high = max(begin, TOP), min(begin + rows, FRAME1 - 1)
                for part in range(PARTS):
                    field[part, low:high] = ref[(*at, part, slice(low - begin, high - begin))]

    packed_edges = field[4]
    lane = lanes_of((FRAME1, LANES))
    edges = {}
    for place, part in enumerate(EDGED):
        edges[part] = jnp.where(lane < 64, pltpu.roll(packed_edges, (LANES - place) % LANES, 1), pltpu.roll(packed_edges, place, 1)) if place else packed_edges
    for begin, rate, running in ((0, field[3], field[2]), (KINDS, edges[3], edges[2])):
        quotient = running / rate
        for kind in range(KINDS):
            factor = jnp.exp(rate * (-time_step * (LEAST + kind)))
            factors[begin + kind] = factor
            reliefs[begin + kind] = (1.0 - factor) * quotient * (1.0 / SCALE)
    cost[...] = field[2] * (0.5 / SCALE)

    def opening(j, now):
        density, value, edge = now
        back = SLICES - 1 - j
        m0[j] = density
        u0[back] = value
        e0[back] = edge
        kind = table[SLICES + back] - LEAST
        density = factors[table[SLICES + j] - LEAST] * density
        value = factors[kind] * value + reliefs[kind]
        edge = factors[KINDS + kind] * edge + reliefs[KINDS + kind]
        return density, value, edge

    lax.fori_loop(0, SLICES, opening, (field[0], field[1] * (1.0 / SCALE), edges[1] * (1.0 / SCALE)), unroll=2)

    fine_groups(GROUP1, table, u0, e0, m0, planes_of(cost, (), 7, 9), sources, across, along, (va, vb), (da, db), fu, fm, ((7, 9), (15, 7)))

    inner = pl.ds(16, FRAME2)

    def first_sweep(j, now):
        density, value = now
        back = SLICES - 1 - j
        m1[j] = density
        u1[back] = value
        density = factors[table[SLICES + j] - LEAST, inner] * (density - m0[j, inner]) + fm[j, inner]
        value = factors[table[SLICES + back] - LEAST, inner] * (value - u0[back, inner]) + fu[back, inner]
        return density, value

    lax.fori_loop(0, SLICES, first_sweep, (field[0, inner], field[1, inner] * (1.0 / SCALE)), unroll=4)

    fine_groups(GROUP2, table, u1, None, m1, planes_of(cost, (), 23, 5), sources, across, along, (va, vb), (da, db), fu, fm, ((7, 5), (15, 3)))

    tile, wide = pl.ds(24, 8), pl.ds(40, 8)

    def second_sweep(j, now):
        density, value = now
        back = SLICES - 1 - j
        u0[back, 0:8] = value
        m0[j, 0:8] = density
        density = factors[table[SLICES + j] - LEAST, wide] * (density - m1[j, tile]) + fm[j, tile]
        value = factors[table[SLICES + back] - LEAST, wide] * (value - u1[back, tile]) + fu[back, tile]
        return density, value

    lax.fori_loop(0, SLICES, second_sweep, (field[0, wide], field[1, wide] * (1.0 / SCALE)), unroll=8)

    lane = lanes_of((8, LANES))
    first_half = lane < HALF
    wanted = COL_AT // 2 + lane % HALF // 2 + HALF * (lane % 2)
    for j in range(SLICES):
        density, value = m0[j, 0:8], SCALE * u0[j, 0:8]
        ahead, behind = jnp.where(half == 0, density, value), jnp.where(half == 0, value, density)
        message[j] = jnp.where(first_half, jnp.take_along_axis(ahead, wanted, 1), jnp.take_along_axis(behind, wanted, 1))


def place_of():
    zh, x, c = (lax.axis_index(axis) for axis in TM)
    return 2 * c + x % 2, 2 * zh + x // 2, x // 2, c


def window_kernel(*refs):
    arrays, (near, far), (blocks, arrived) = refs[:4], refs[4:6], refs[6:]
    _, column, _, core = place_of()
    begin = (column * TILE_COLS + 512 - COL_AT) % 512
    first, shift = begin // LANES, LANES - begin % LANES
    copies = []
    for part, array in enumerate(arrays):
        for which in range(2):
            at = pl.multiple_of(((first + which) % 4) * LANES, LANES)
            copies.append(pltpu.make_async_copy(array.at[:, pl.ds(at, LANES)], blocks.at[part, which], arrived.at[part, which]))
    for copy in copies:
        copy.start()
    for copy in copies:
        copy.wait()
    lane = lanes_of((ROWS, LANES))
    beside = jnp.zeros((ROWS, LANES), jnp.float32)
    for part in range(PARTS):
        if part < 4:
            a, b = blocks[part, 0], blocks[part, 1]
            window = jnp.where(lane < shift, pltpu.roll(a, shift, 1), pltpu.roll(b, shift, 1))
            window = jnp.take_along_axis(window, lane % HALF * 2 + lane // HALF, 1)
        else:
            window = beside
        near[part] = window

        @pl.when(core == 0)
        def _(window=window, part=part):
            far[part] = window[8:24]

        @pl.when(core != 0)
        def _(window=window, part=part):
            far[part] = window[0:16]

        if part in EDGED:
            place = EDGED.index(part)
            beside = jnp.where(lane == place, pltpu.roll(a, shift + 1 + place, 1), beside)
            beside = jnp.where(lane == LANES - 1 - place, pltpu.roll(b, shift - 1 - place, 1), beside)


def gather_kernel(received, density, value):
    first_half = lanes_of((8, LANES)) < 64
    for zh in range(4):
        for band in range(4):
            at = [zh * 8 + (2 * half + band % 2) * 2 + band // 2 for half in range(2)]
            a, b = received[at[0]], received[at[1]]
            rows, lanes = slice(TILE_ROWS * band, TILE_ROWS * (band + 1)), slice(LANES * zh, LANES * (zh + 1))
            density[0, rows, lanes] = jnp.where(first_half, a, b)[0:TILE_ROWS]
            value[0, rows, lanes] = pltpu.roll(jnp.where(first_half, b, a), 64, 1)[0:TILE_ROWS]


def vmem():
    return pl.BlockSpec(memory_space=pltpu.VMEM)


def smem():
    return pl.BlockSpec(memory_space=pltpu.SMEM)


def f32(*shape):
    return jax.ShapeDtypeStruct(shape, jnp.float32)


def windows(*arrays):
    return pl.pallas_call(
        window_kernel,
        out_shape=[f32(PARTS, ROWS, LANES), f32(PARTS, 16, LANES)],
        in_specs=[pl.BlockSpec(memory_space=pl.ANY)] * 4,
        out_specs=[vmem(), vmem()],
        scratch_shapes=[pltpu.VMEM((4, 2, ROWS, LANES), jnp.float32), pltpu.SemaphoreType.DMA((4, 2))],
        name="windows",
    )(*arrays)


def both_iterations(table, own, near, far):
    scratch = [
        (PARTS, FRAME1, LANES),
        (2 * KINDS, FRAME1, LANES),
        (2 * KINDS, FRAME1, LANES),
        (FRAME1, LANES),
        (SLICES, FRAME1, LANES),
        (SLICES, FRAME1, LANES),
        (SLICES, FRAME1, LANES),
        (SLICES, FRAME2, LANES),
        (SLICES, FRAME2, LANES),
        (SLICES, FRAME1, LANES),
        (SLICES, FRAME1, LANES),
        (GROUP, K + 1, FRAME1, LANES),
        (GROUP, K + 1, FRAME1, LANES),
        (PAIRS, 2, 9, 8, LANES),
        (PAIRS, 2, 9, 8, LANES),
        (PAIRS, 2, 9, 8, LANES),
        (PAIRS, 2, 9, 8, LANES),
        (PAIRS, 2, 9, 8, LANES),
    ]
    return pl.pallas_call(
        main_kernel,
        out_shape=f32(SLICES, 8, LANES),
        in_specs=[smem(), vmem(), vmem(), vmem()],
        out_specs=vmem(),
        scratch_shapes=[pltpu.VMEM(shape, jnp.float32) for shape in scratch],
        compiler_params=pltpu.CompilerParams(vmem_limit_bytes=32 * 2**20),
        name="both_iterations",
    )(table, own, near, far)


def gathered(received):
    return pl.pallas_call(
        gather_kernel,
        out_shape=[f32(1, ROWS, 512), f32(1, ROWS, 512)],
        in_specs=[vmem()],
        out_specs=[vmem(), vmem()],
        compiler_params=pltpu.CompilerParams(vmem_limit_bytes=2 * 2**20),
        name="gathered",
    )(received)


def toward_own_side(array, distance):
    hops = []
    for c in range(2):
        for space in range(16):
            source = (space + (distance if c else -distance)) % 16
            hops.append((c * 16 + source, c * 16 + space))
    return lax.ppermute(array, ("c", *SPACE), hops)


def on_device(initial_density, terminal_cost, running_cost, discount_rate, slice_steps):
    own, edge = windows(initial_density, terminal_cost, running_cost, discount_rate)
    beside = toward_own_side(own, 1)
    near = lax.all_gather(beside, "c")
    band, _, half, _ = place_of()
    numbers = jnp.arange(SLICES, dtype=jnp.int32)
    ahead = (slice_steps[None, :] < slice_steps[:, None]) | ((slice_steps[None, :] == slice_steps[:, None]) & (numbers[None, :] < numbers[:, None]))
    rank = jnp.sum(ahead.astype(jnp.int32), axis=1)
    order = jnp.sum(jnp.where(rank[None, :] == numbers[:, None], numbers[None, :], 0), axis=1)
    table = jnp.concatenate([order, slice_steps, jnp.stack([band, half]).astype(jnp.int32)])
    edge, table = lax.optimization_barrier((edge, table))
    far = toward_own_side(edge, 2)
    message = both_iterations(table, own, near, far)
    received = lax.all_to_all(message, TM, 0, 0, tiled=True)
    return tuple(gathered(received))


def solution(mesh):
    finer = Mesh(mesh.devices.reshape(4, 4, 2, 8, 2), ("zh", "x", "c", "y", "zl"))
    placed = (P(SPACE, None), P(SPACE, None), P(SPACE, None), P(SPACE, None), P())
    return jax.shard_map(
        on_device,
        mesh=finer,
        in_specs=placed,
        out_specs=(P(TM, SPACE, None), P(TM, SPACE, None)),
        check_vma=False,
    )
```

```python
import jax
import jax.numpy as jnp
from jax import lax
from jax.experimental import pallas as pl
from jax.experimental.pallas import tpu as pltpu
from jax.sharding import Mesh
from jax.sharding import PartitionSpec as P


K = 8
SLICES = 32
LEAST = 4
KINDS = K - LEAST + 1
GROUP1 = 16
GROUP2 = 16
GROUP = max(GROUP1, GROUP2)
PAIRS = GROUP // 2
HALF = 64
TM = ("zh", "x", "c")
SPACE = ("y", "zl")

time_step = 0.05
diffusion = 2.0
coupling = 0.1

ROWS = 24
TILE_ROWS = 6
TILE_COLS = 64
LANES = 128
COL_AT = 32
FRAME1 = 80
FRAME2 = 48
TOP = 7
PARTS = 5
EDGED = (1, 2, 3)
SCALE = 16.0


def planes_of(ref, at, start, count):
    return [ref[(*at, pl.ds(start + k, 8, stride=count), slice(None))] for k in range(count)]


def put_planes(ref, at, start, planes):
    count = len(planes)
    for k, plane in enumerate(planes):
        ref[(*at, pl.ds(start + k, 8, stride=count), slice(None))] = plane


def row_above(planes):
    return [pltpu.roll(planes[-1], 1, 0), *planes[:-1]]


def row_below(planes):
    return [*planes[1:], pltpu.roll(planes[0], 7, 0)]


def left(plane):
    return pltpu.roll(plane, 1, 1)


def right(plane):
    return pltpu.roll(plane, LANES - 1, 1)


def lanes_of(shape):
    return lax.broadcasted_iota(jnp.int32, shape, len(shape) - 1)


def paired(a, b):
    first = lanes_of(a.shape) < HALF
    return jnp.where(first, a, pltpu.roll(b, HALF, 1)), jnp.where(first, pltpu.roll(a, HALF, 1), b)


def pair_planes(many_a, many_b):
    both = [paired(a, b) for a, b in zip(many_a, many_b)]
    return [even for even, _ in both], [odd for _, odd in both]


def slope_planes(even, odd, beside=None):
    result = []
    for parity, planes in enumerate((even, odd)):
        up, down = row_above(planes), row_below(planes)
        slopes, sums = [], []
        for k in range(len(planes)):
            if parity == 0:
                west, east = left(odd[k]), odd[k]
                if beside is not None:
                    west = jnp.where(lanes_of(west.shape) % HALF == 0, beside[0][k], west)
            else:
                west, east = even[k], right(even[k])
                if beside is not None:
                    east = jnp.where(lanes_of(east.shape) % HALF == HALF - 1, beside[1][k], east)
            slopes.append((down[k] - up[k], east - west))
            sums.append((up[k] + down[k]) + (west + east))
        result.append((planes, slopes, sums))
    return result


def fine_groups(size, table, values, beside, densities, cost, sources, across, along, value_now, density_now, out_value, out_density, spots):
    (value_at, value_n), (density_at, density_n) = spots
    keep_all, share_all = 1.0 - 4.0 * time_step * diffusion, time_step * diffusion
    costs = pair_planes(cost, cost)
    first = lanes_of((8, LANES)) < HALF

    def group(number, carry):
        own = [table[size * number + h] for h in range(size)]
        trips = [table[SLICES + j] for j in own]
        most = trips[-1]

        def taken(ref, at, n, h):
            return pair_planes(*[planes_of(ref, (own[2 * h + side],), at, n) for side in range(2)])

        def left_at(ref, at, h, both):
            for side, planes in enumerate(pair_planes(*both)):
                put_planes(ref, (own[2 * h + side],), at, planes)

        def weights(h, test):
            on = [test(trips[2 * h + side]) for side in range(2)]
            keep = jnp.where(first, jnp.where(on[0], keep_all, 1.0), jnp.where(on[1], keep_all, 1.0))
            share = jnp.where(first, jnp.where(on[0], share_all, 0.0), jnp.where(on[1], share_all, 0.0))
            return keep, share

        for h in range(size // 2):
            start, held, density = taken(values, value_at, value_n, h), taken(densities, value_at, value_n, h), taken(densities, density_at, density_n, h)
            for parity in range(2):
                for k in range(value_n):
                    value_now[0][h, parity, k] = value_now[1][h, parity, k] = start[parity][k]
                    sources[h, parity, k] = costs[parity][k] + (0.5 / SCALE * coupling) * held[parity][k]
                for k in range(density_n):
                    density_now[0][h, parity, k] = density[parity][k]

        def slopes_of(q, h):
            now = [[value_now[q % 2][h, parity, k] for k in range(value_n)] for parity in range(2)]
            edges = taken(beside, value_at, value_n, h) if q == 0 and beside is not None else None
            result = slope_planes(*now, edges)
            for parity in range(2):
                put_planes(across, (2 * h + parity, q), value_at, [a for a, _ in result[parity][1]])
                put_planes(along, (2 * h + parity, q), value_at, [b for _, b in result[parity][1]])
            return result

        def value_step(q):
            for h in range(size // 2):
                keep, share = keep_all, share_all
                if q < K - LEAST:
                    keep, share = weights(h, lambda count: q >= K - count)
                for parity, (now, slopes, sums) in enumerate(slopes_of(q, h)):
                    for k in range(value_n):
                        a, b = slopes[k]
                        value_now[1 - q % 2][h, parity, k] = keep * now[k] + share * (sums[k] + (sources[h, parity, k] - (a * a + b * b)))

        def density_step(i):
            for h in range(size // 2):
                keep, share = keep_all, share_all
                if i >= LEAST:
                    keep, share = weights(h, lambda count: i < count)
                here, rows, more, less = [], [], [], []
                for parity in range(2):
                    a = planes_of(across, (2 * h + parity, K - i), density_at, density_n)
                    b = planes_of(along, (2 * h + parity, K - i), density_at, density_n)
                    now = [density_now[i % 2][h, parity, k] for k in range(density_n)]
                    twice = [plane + plane for plane in now]
                    flux = [twice[k] * a[k] for k in range(density_n)]
                    below = row_below([now[k] + flux[k] for k in range(density_n)])
                    above = row_above([now[k] - flux[k] for k in range(density_n)])
                    drift = [twice[k] * b[k] for k in range(density_n)]
                    here.append(now)
                    rows.append([below[k] + above[k] for k in range(density_n)])
                    more.append([now[k] + drift[k] for k in range(density_n)])
                    less.append([now[k] - drift[k] for k in range(density_n)])
                for k in range(density_n):
                    around = (rows[0][k] + more[1][k]) + left(less[1][k]), (rows[1][k] + less[0][k]) + right(more[0][k])
                    for parity in range(2):
                        density_now[1 - i % 2][h, parity, k] = keep * here[parity][k] + share * around[parity]

        for q in range(K):
            if q < K - LEAST:
                pl.when(q >= K - most)(lambda q=q: value_step(q))
            else:
                value_step(q)
        for h in range(size // 2):
            left_at(out_value, value_at, h, [planes for planes, _, _ in slopes_of(K, h)])
        for i in range(K):
            if i >= LEAST:
                pl.when(i < most)(lambda i=i: density_step(i))
            else:
                density_step(i)
        for last in range(2):

            @pl.when(most % 2 == last)
            def _(last=last):
                for h in range(size // 2):
                    left_at(out_density, density_at, h, [[density_now[last][h, parity, k] for k in range(density_n)] for parity in range(2)])

        return carry

    lax.fori_loop(0, SLICES // size, group, 0)


def main_kernel(table, own, near, far, message, field, factors, reliefs, cost, m0, u0, e0, m1, u1, fm, fu, across, along, sources, va, vb, da, db):
    band, half = table[2 * SLICES], table[2 * SLICES + 1]
    for position in range(4):

        @pl.when(band == position)
        def _(position=position):
            pieces = [(near, (0,), ROWS, -24), (own, (), ROWS, 0), (near, (1,), ROWS, 24), (far, (), 16, -40 if position < 2 else 48)]
            for ref, at, rows, first in pieces:
                begin = first - TILE_ROWS * position + 40
                low, high = max(begin, TOP), min(begin + rows, FRAME1 - 1)
                for part in range(PARTS):
                    field[part, low:high] = ref[(*at, part, slice(low - begin, high - begin))]

    packed_edges = field[4]
    lane = lanes_of((FRAME1, LANES))
    edges = {}
    for place, part in enumerate(EDGED):
        edges[part] = jnp.where(lane < 64, pltpu.roll(packed_edges, (LANES - place) % LANES, 1), pltpu.roll(packed_edges, place, 1)) if place else packed_edges
    for begin, rate, running in ((0, field[3], field[2]), (KINDS, edges[3], edges[2])):
        quotient = running / rate
        for kind in range(KINDS):
            factor = jnp.exp(rate * (-time_step * (LEAST + kind)))
            factors[begin + kind] = factor
            reliefs[begin + kind] = (1.0 - factor) * quotient * (1.0 / SCALE)
    cost[...] = field[2] * (0.5 / SCALE)

    def opening(j, now):
        density, value, edge = now
        back = SLICES - 1 - j
        m0[j] = density
        u0[back] = value
        e0[back] = edge
        kind = table[SLICES + back] - LEAST
        density = factors[table[SLICES + j] - LEAST] * density
        value = factors[kind] * value + reliefs[kind]
        edge = factors[KINDS + kind] * edge + reliefs[KINDS + kind]
        return density, value, edge

    lax.fori_loop(0, SLICES, opening, (field[0], field[1] * (1.0 / SCALE), edges[1] * (1.0 / SCALE)), unroll=2)

    fine_groups(GROUP1, table, u0, e0, m0, planes_of(cost, (), 7, 9), sources, across, along, (va, vb), (da, db), fu, fm, ((7, 9), (15, 7)))

    inner = pl.ds(16, FRAME2)

    def first_sweep(j, now):
        density, value = now
        back = SLICES - 1 - j
        m1[j] = density
        u1[back] = value
        density = factors[table[SLICES + j] - LEAST, inner] * (density - m0[j, inner]) + fm[j, inner]
        value = factors[table[SLICES + back] - LEAST, inner] * (value - u0[back, inner]) + fu[back, inner]
        return density, value

    lax.fori_loop(0, SLICES, first_sweep, (field[0, inner], field[1, inner] * (1.0 / SCALE)), unroll=4)

    fine_groups(GROUP2, table, u1, None, m1, planes_of(cost, (), 23, 5), sources, across, along, (va, vb), (da, db), fu, fm, ((7, 5), (15, 3)))

    tile, wide = pl.ds(24, 8), pl.ds(40, 8)

    def second_sweep(j, now):
        density, value = now
        back = SLICES - 1 - j
        u0[back, 0:8] = value
        m0[j, 0:8] = density
        density = factors[table[SLICES + j] - LEAST, wide] * (density - m1[j, tile]) + fm[j, tile]
        value = factors[table[SLICES + back] - LEAST, wide] * (value - u1[back, tile]) + fu[back, tile]
        return density, value

    lax.fori_loop(0, SLICES, second_sweep, (field[0, wide], field[1, wide] * (1.0 / SCALE)), unroll=8)

    lane = lanes_of((8, LANES))
    first_half = lane < HALF
    wanted = COL_AT // 2 + lane % HALF // 2 + HALF * (lane % 2)
    for j in range(SLICES):
        density, value = m0[j, 0:8], SCALE * u0[j, 0:8]
        ahead, behind = jnp.where(half == 0, density, value), jnp.where(half == 0, value, density)
        whole = jnp.where(first_half, jnp.take_along_axis(ahead, wanted, 1), jnp.take_along_axis(behind, wanted, 1))
        message[j] = whole[0:TILE_ROWS]


def place_of():
    zh, x, c = (lax.axis_index(axis) for axis in TM)
    return 2 * c + x % 2, 2 * zh + x // 2, x // 2, c


def window_kernel(*refs):
    arrays, (near, far), (blocks, arrived) = refs[:4], refs[4:6], refs[6:]
    _, column, _, core = place_of()
    begin = (column * TILE_COLS + 512 - COL_AT) % 512
    first, shift = begin // LANES, LANES - begin % LANES
    copies = []
    for part, array in enumerate(arrays):
        for which in range(2):
            at = pl.multiple_of(((first + which) % 4) * LANES, LANES)
            copies.append(pltpu.make_async_copy(array.at[:, pl.ds(at, LANES)], blocks.at[part, which], arrived.at[part, which]))
    for copy in copies:
        copy.start()
    for copy in copies:
        copy.wait()
    lane = lanes_of((ROWS, LANES))
    beside = jnp.zeros((ROWS, LANES), jnp.float32)
    for part in range(PARTS):
        if part < 4:
            a, b = blocks[part, 0], blocks[part, 1]
            window = jnp.where(lane < shift, pltpu.roll(a, shift, 1), pltpu.roll(b, shift, 1))
            window = jnp.take_along_axis(window, lane % HALF * 2 + lane // HALF, 1)
        else:
            window = beside
        near[part] = window

        @pl.when(core == 0)
        def _(window=window, part=part):
            far[part] = window[8:24]

        @pl.when(core != 0)
        def _(window=window, part=part):
            far[part] = window[0:16]

        if part in EDGED:
            place = EDGED.index(part)
            beside = jnp.where(lane == place, pltpu.roll(a, shift + 1 + place, 1), beside)
            beside = jnp.where(lane == LANES - 1 - place, pltpu.roll(b, shift - 1 - place, 1), beside)


def gather_kernel(received, density, value):
    first_half = lanes_of((TILE_ROWS, LANES)) < 64
    for zh in range(4):
        for band in range(4):
            at = [zh * 8 + (2 * half + band % 2) * 2 + band // 2 for half in range(2)]
            a, b = received[at[0]], received[at[1]]
            rows, lanes = slice(TILE_ROWS * band, TILE_ROWS * (band + 1)), slice(LANES * zh, LANES * (zh + 1))
            density[0, rows, lanes] = jnp.where(first_half, a, b)
            value[0, rows, lanes] = pltpu.roll(jnp.where(first_half, b, a), 64, 1)


def vmem():
    return pl.BlockSpec(memory_space=pltpu.VMEM)


def smem():
    return pl.BlockSpec(memory_space=pltpu.SMEM)


def f32(*shape):
    return jax.ShapeDtypeStruct(shape, jnp.float32)


def windows(*arrays):
    return pl.pallas_call(
        window_kernel,
        out_shape=[f32(PARTS, ROWS, LANES), f32(PARTS, 16, LANES)],
        in_specs=[pl.BlockSpec(memory_space=pl.ANY)] * 4,
        out_specs=[vmem(), vmem()],
        scratch_shapes=[pltpu.VMEM((4, 2, ROWS, LANES), jnp.float32), pltpu.SemaphoreType.DMA((4, 2))],
        name="windows",
    )(*arrays)


def both_iterations(table, own, near, far):
    scratch = [
        (PARTS, FRAME1, LANES),
        (2 * KINDS, FRAME1, LANES),
        (2 * KINDS, FRAME1, LANES),
        (FRAME1, LANES),
        (SLICES, FRAME1, LANES),
        (SLICES, FRAME1, LANES),
        (SLICES, FRAME1, LANES),
        (SLICES, FRAME2, LANES),
        (SLICES, FRAME2, LANES),
        (SLICES, FRAME1, LANES),
        (SLICES, FRAME1, LANES),
        (GROUP, K + 1, FRAME1, LANES),
        (GROUP, K + 1, FRAME1, LANES),
        (PAIRS, 2, 9, 8, LANES),
        (PAIRS, 2, 9, 8, LANES),
        (PAIRS, 2, 9, 8, LANES),
        (PAIRS, 2, 9, 8, LANES),
        (PAIRS, 2, 9, 8, LANES),
    ]
    return pl.pallas_call(
        main_kernel,
        out_shape=f32(SLICES, TILE_ROWS, LANES),
        in_specs=[smem(), vmem(), vmem(), vmem()],
        out_specs=vmem(),
        scratch_shapes=[pltpu.VMEM(shape, jnp.float32) for shape in scratch],
        compiler_params=pltpu.CompilerParams(vmem_limit_bytes=32 * 2**20),
        name="both_iterations",
    )(table, own, near, far)


def gathered(received):
    return pl.pallas_call(
        gather_kernel,
        out_shape=[f32(1, ROWS, 512), f32(1, ROWS, 512)],
        in_specs=[vmem()],
        out_specs=[vmem(), vmem()],
        compiler_params=pltpu.CompilerParams(vmem_limit_bytes=2 * 2**20),
        name="gathered",
    )(received)


def toward_own_side(array, distance):
    hops = []
    for c in range(2):
        for space in range(16):
            source = (space + (distance if c else -distance)) % 16
            hops.append((c * 16 + source, c * 16 + space))
    return lax.ppermute(array, ("c", *SPACE), hops)


def on_device(initial_density, terminal_cost, running_cost, discount_rate, slice_steps):
    own, edge = windows(initial_density, terminal_cost, running_cost, discount_rate)
    beside = toward_own_side(own, 1)
    near = lax.all_gather(beside, "c")
    band, _, half, _ = place_of()
    numbers = jnp.arange(SLICES, dtype=jnp.int32)
    ahead = (slice_steps[None, :] < slice_steps[:, None]) | ((slice_steps[None, :] == slice_steps[:, None]) & (numbers[None, :] < numbers[:, None]))
    rank = jnp.sum(ahead.astype(jnp.int32), axis=1)
    order = jnp.sum(jnp.where(rank[None, :] == numbers[:, None], numbers[None, :], 0), axis=1)
    table = jnp.concatenate([order, slice_steps, jnp.stack([band, half]).astype(jnp.int32)])
    edge, table = lax.optimization_barrier((edge, table))
    far = toward_own_side(edge, 2)
    message = both_iterations(table, own, near, far)
    received = lax.all_to_all(message, TM, 0, 0, tiled=True)
    return tuple(gathered(received))


def solution(mesh):
    finer = Mesh(mesh.devices.reshape(4, 4, 2, 8, 2), ("zh", "x", "c", "y", "zl"))
    placed = (P(SPACE, None), P(SPACE, None), P(SPACE, None), P(SPACE, None), P())
    return jax.shard_map(
        on_device,
        mesh=finer,
        in_specs=placed,
        out_specs=(P(TM, SPACE, None), P(TM, SPACE, None)),
        check_vma=False,
    )
```

```python
import jax
import jax.numpy as jnp
from jax import lax
from jax.experimental import pallas as pl
from jax.experimental.pallas import tpu as pltpu
from jax.sharding import Mesh
from jax.sharding import PartitionSpec as P


K = 8
SLICES = 32
LEAST = 4
KINDS = K - LEAST + 1
GROUP1 = 16
GROUP2 = 16
GROUP = max(GROUP1, GROUP2)
PAIRS = GROUP // 2
HALF = 64
TM = ("zh", "x", "c")
SPACE = ("y", "zl")

time_step = 0.05
diffusion = 2.0
coupling = 0.1

ROWS = 24
TILE_ROWS = 6
TILE_COLS = 64
LANES = 128
COL_AT = 32
FRAME1 = 80
FRAME2 = 48
TOP = 7
PARTS = 5
EDGED = (1, 2, 3)
SCALE = 16.0


def planes_of(ref, at, start, count):
    return [ref[(*at, pl.ds(start + k, 8, stride=count), slice(None))] for k in range(count)]


def put_planes(ref, at, start, planes):
    count = len(planes)
    for k, plane in enumerate(planes):
        ref[(*at, pl.ds(start + k, 8, stride=count), slice(None))] = plane


def row_above(planes):
    return [pltpu.roll(planes[-1], 1, 0), *planes[:-1]]


def row_below(planes):
    return [*planes[1:], pltpu.roll(planes[0], 7, 0)]


def left(plane):
    return pltpu.roll(plane, 1, 1)


def right(plane):
    return pltpu.roll(plane, LANES - 1, 1)


def lanes_of(shape):
    return lax.broadcasted_iota(jnp.int32, shape, len(shape) - 1)


def paired(a, b):
    first = lanes_of(a.shape) < HALF
    return jnp.where(first, a, pltpu.roll(b, HALF, 1)), jnp.where(first, pltpu.roll(a, HALF, 1), b)


def pair_planes(many_a, many_b):
    both = [paired(a, b) for a, b in zip(many_a, many_b)]
    return [even for even, _ in both], [odd for _, odd in both]


def slope_planes(even, odd, beside=None):
    result = []
    for parity, planes in enumerate((even, odd)):
        up, down = row_above(planes), row_below(planes)
        slopes, sums = [], []
        for k in range(len(planes)):
            if parity == 0:
                west, east = left(odd[k]), odd[k]
                if beside is not None:
                    west = jnp.where(lanes_of(west.shape) % HALF == 0, beside[0][k], west)
            else:
                west, east = even[k], right(even[k])
                if beside is not None:
                    east = jnp.where(lanes_of(east.shape) % HALF == HALF - 1, beside[1][k], east)
            slopes.append((down[k] - up[k], east - west))
            sums.append((up[k] + down[k]) + (west + east))
        result.append((planes, slopes, sums))
    return result


def fine_groups(size, table, values, beside, densities, cost, sources, across, along, value_now, density_now, out_value, out_density, spots):
    (value_at, value_n), (density_at, density_n) = spots
    keep_all, share_all = 1.0 - 4.0 * time_step * diffusion, time_step * diffusion
    costs = pair_planes(cost, cost)
    first = lanes_of((8, LANES)) < HALF

    def group(number, carry):
        own = [table[size * number + h] for h in range(size)]
        trips = [table[SLICES + j] for j in own]
        most = trips[-1]

        def taken(ref, at, n, h):
            return pair_planes(*[planes_of(ref, (own[2 * h + side],), at, n) for side in range(2)])

        def left_at(ref, at, h, both):
            for side, planes in enumerate(pair_planes(*both)):
                put_planes(ref, (own[2 * h + side],), at, planes)

        def weights(h, test):
            on = [test(trips[2 * h + side]) for side in range(2)]
            keep = jnp.where(first, jnp.where(on[0], keep_all, 1.0), jnp.where(on[1], keep_all, 1.0))
            share = jnp.where(first, jnp.where(on[0], share_all, 0.0), jnp.where(on[1], share_all, 0.0))
            return keep, share

        for h in range(size // 2):
            start, held, density = taken(values, value_at, value_n, h), taken(densities, value_at, value_n, h), taken(densities, density_at, density_n, h)
            for parity in range(2):
                for k in range(value_n):
                    value_now[0][h, parity, k] = value_now[1][h, parity, k] = start[parity][k]
                    sources[h, parity, k] = costs[parity][k] + (0.5 / SCALE * coupling) * held[parity][k]
                for k in range(density_n):
                    density_now[0][h, parity, k] = density[parity][k]

        def slopes_of(q, h):
            now = [[value_now[q % 2][h, parity, k] for k in range(value_n)] for parity in range(2)]
            edges = taken(beside, value_at, value_n, h) if q == 0 and beside is not None else None
            result = slope_planes(*now, edges)
            for parity in range(2):
                put_planes(across, (2 * h + parity, q), value_at, [a for a, _ in result[parity][1]])
                put_planes(along, (2 * h + parity, q), value_at, [b for _, b in result[parity][1]])
            return result

        def value_step(q):
            for h in range(size // 2):
                keep, share = keep_all, share_all
                if q < K - LEAST:
                    keep, share = weights(h, lambda count: q >= K - count)
                for parity, (now, slopes, sums) in enumerate(slopes_of(q, h)):
                    for k in range(value_n):
                        a, b = slopes[k]
                        value_now[1 - q % 2][h, parity, k] = keep * now[k] + share * (sums[k] + (sources[h, parity, k] - (a * a + b * b)))

        def density_step(i):
            for h in range(size // 2):
                keep, share = keep_all, share_all
                if i >= LEAST:
                    keep, share = weights(h, lambda count: i < count)
                here, rows, more, less = [], [], [], []
                for parity in range(2):
                    a = planes_of(across, (2 * h + parity, K - i), density_at, density_n)
                    b = planes_of(along, (2 * h + parity, K - i), density_at, density_n)
                    now = [density_now[i % 2][h, parity, k] for k in range(density_n)]
                    twice = [plane + plane for plane in now]
                    flux = [twice[k] * a[k] for k in range(density_n)]
                    below = row_below([now[k] + flux[k] for k in range(density_n)])
                    above = row_above([now[k] - flux[k] for k in range(density_n)])
                    drift = [twice[k] * b[k] for k in range(density_n)]
                    here.append(now)
                    rows.append([below[k] + above[k] for k in range(density_n)])
                    more.append([now[k] + drift[k] for k in range(density_n)])
                    less.append([now[k] - drift[k] for k in range(density_n)])
                for k in range(density_n):
                    around = (rows[0][k] + more[1][k]) + left(less[1][k]), (rows[1][k] + less[0][k]) + right(more[0][k])
                    for parity in range(2):
                        density_now[1 - i % 2][h, parity, k] = keep * here[parity][k] + share * around[parity]

        for q in range(K):
            if q < K - LEAST:
                pl.when(q >= K - most)(lambda q=q: value_step(q))
            else:
                value_step(q)
        for h in range(size // 2):
            left_at(out_value, value_at, h, [planes for planes, _, _ in slopes_of(K, h)])
        for i in range(K):
            if i >= LEAST:
                pl.when(i < most)(lambda i=i: density_step(i))
            else:
                density_step(i)
        for last in range(2):

            @pl.when(most % 2 == last)
            def _(last=last):
                for h in range(size // 2):
                    left_at(out_density, density_at, h, [[density_now[last][h, parity, k] for k in range(density_n)] for parity in range(2)])

        return carry

    lax.fori_loop(0, SLICES // size, group, 0)


def main_kernel(table, own, near, far, message, field, factors, reliefs, cost, m0, u0, e0, m1, u1, fm, fu, across, along, sources, va, vb, da, db):
    band, half = table[2 * SLICES], table[2 * SLICES + 1]
    for position in range(4):

        @pl.when(band == position)
        def _(position=position):
            pieces = [(near, (0,), ROWS, -24), (own, (), ROWS, 0), (near, (1,), ROWS, 24), (far, (), 16, -40 if position < 2 else 48)]
            for ref, at, rows, first in pieces:
                begin = first - TILE_ROWS * position + 40
                low, high = max(begin, TOP), min(begin + rows, FRAME1 - 1)
                for part in range(PARTS):
                    field[part, low:high] = ref[(*at, part, slice(low - begin, high - begin))]

    packed_edges = field[4]
    lane = lanes_of((FRAME1, LANES))
    edges = {}
    for place, part in enumerate(EDGED):
        edges[part] = jnp.where(lane < 64, pltpu.roll(packed_edges, (LANES - place) % LANES, 1), pltpu.roll(packed_edges, place, 1)) if place else packed_edges
    for begin, rate, running in ((0, field[3], field[2]), (KINDS, edges[3], edges[2])):
        quotient = running / rate
        for kind in range(KINDS):
            factor = jnp.exp(rate * (-time_step * (LEAST + kind)))
            factors[begin + kind] = factor
            reliefs[begin + kind] = (1.0 - factor) * quotient * (1.0 / SCALE)
    cost[...] = field[2] * (0.5 / SCALE)

    def opening(j, now):
        density, value, edge = now
        back = SLICES - 1 - j
        m0[j] = density
        u0[back] = value
        e0[back] = edge
        kind = table[SLICES + back] - LEAST
        density = factors[table[SLICES + j] - LEAST] * density
        value = factors[kind] * value + reliefs[kind]
        edge = factors[KINDS + kind] * edge + reliefs[KINDS + kind]
        return density, value, edge

    lax.fori_loop(0, SLICES, opening, (field[0], field[1] * (1.0 / SCALE), edges[1] * (1.0 / SCALE)), unroll=2)

    fine_groups(GROUP1, table, u0, e0, m0, planes_of(cost, (), 7, 9), sources, across, along, (va, vb), (da, db), fu, fm, ((7, 9), (15, 7)))

    inner = pl.ds(16, FRAME2)

    def first_sweep(j, now):
        density, value = now
        back = SLICES - 1 - j
        m1[j] = density
        u1[back] = value
        density = factors[table[SLICES + j] - LEAST, inner] * (density - m0[j, inner]) + fm[j, inner]
        value = factors[table[SLICES + back] - LEAST, inner] * (value - u0[back, inner]) + fu[back, inner]
        return density, value

    lax.fori_loop(0, SLICES, first_sweep, (field[0, inner], field[1, inner] * (1.0 / SCALE)), unroll=4)

    fine_groups(GROUP2, table, u1, None, m1, planes_of(cost, (), 23, 5), sources, across, along, (va, vb), (da, db), fu, fm, ((7, 5), (15, 3)))

    tile, wide = pl.ds(24, 8), pl.ds(40, 8)

    def second_sweep(j, now):
        density, value = now
        back = SLICES - 1 - j
        u0[back, 0:8] = value
        m0[j, 0:8] = density
        density = factors[table[SLICES + j] - LEAST, wide] * (density - m1[j, tile]) + fm[j, tile]
        value = factors[table[SLICES + back] - LEAST, wide] * (value - u1[back, tile]) + fu[back, tile]
        return density, value

    lax.fori_loop(0, SLICES, second_sweep, (field[0, wide], field[1, wide] * (1.0 / SCALE)), unroll=8)

    lane = lanes_of((8, LANES))
    first_half = lane < HALF
    wanted = COL_AT // 2 + lane % HALF // 2 + HALF * (lane % 2)
    for j in range(SLICES):
        density, value = m0[j, 0:8], SCALE * u0[j, 0:8]
        ahead, behind = jnp.where(half == 0, density, value), jnp.where(half == 0, value, density)
        whole = jnp.where(first_half, jnp.take_along_axis(ahead, wanted, 1), jnp.take_along_axis(behind, wanted, 1))
        message[j] = whole[0:TILE_ROWS]


def place_of():
    zh, x, c = (lax.axis_index(axis) for axis in TM)
    return 2 * c + x % 2, 2 * zh + x // 2, x // 2, c


def window_kernel(*refs):
    arrays, (near, far), (blocks, arrived) = refs[:4], refs[4:6], refs[6:]
    _, column, _, core = place_of()
    begin = (column * TILE_COLS + 512 - COL_AT) % 512
    first, shift = begin // LANES, LANES - begin % LANES
    copies = []
    for part, array in enumerate(arrays):
        for which in range(2):
            at = pl.multiple_of(((first + which) % 4) * LANES, LANES)
            copies.append(pltpu.make_async_copy(array.at[:, pl.ds(at, LANES)], blocks.at[part, which], arrived.at[part, which]))
    for copy in copies:
        copy.start()
    for copy in copies:
        copy.wait()
    lane = lanes_of((ROWS, LANES))
    beside = jnp.zeros((ROWS, LANES), jnp.float32)
    for part in range(PARTS):
        if part < 4:
            a, b = blocks[part, 0], blocks[part, 1]
            window = jnp.where(lane < shift, pltpu.roll(a, shift, 1), pltpu.roll(b, shift, 1))
            window = jnp.take_along_axis(window, lane % HALF * 2 + lane // HALF, 1)
        else:
            window = beside
        near[part] = window

        @pl.when(core == 0)
        def _(window=window, part=part):
            far[part] = window[8:24]

        @pl.when(core != 0)
        def _(window=window, part=part):
            far[part] = window[0:16]

        if part in EDGED:
            place = EDGED.index(part)
            beside = jnp.where(lane == place, pltpu.roll(a, shift + 1 + place, 1), beside)
            beside = jnp.where(lane == LANES - 1 - place, pltpu.roll(b, shift - 1 - place, 1), beside)


def gather_kernel(received, density, value):
    first_half = lanes_of((TILE_ROWS, LANES)) < 64
    for zh in range(4):
        for band in range(4):
            at = [zh * 8 + (2 * half + band % 2) * 2 + band // 2 for half in range(2)]
            a, b = received[at[0]], received[at[1]]
            rows, lanes = slice(TILE_ROWS * band, TILE_ROWS * (band + 1)), slice(LANES * zh, LANES * (zh + 1))
            density[0, rows, lanes] = jnp.where(first_half, a, b)
            value[0, rows, lanes] = pltpu.roll(jnp.where(first_half, b, a), 64, 1)


def vmem():
    return pl.BlockSpec(memory_space=pltpu.VMEM)


def smem():
    return pl.BlockSpec(memory_space=pltpu.SMEM)


def f32(*shape):
    return jax.ShapeDtypeStruct(shape, jnp.float32)


def windows(*arrays):
    return pl.pallas_call(
        window_kernel,
        out_shape=[f32(PARTS, ROWS, LANES), f32(PARTS, 16, LANES)],
        in_specs=[pl.BlockSpec(memory_space=pl.ANY)] * 4,
        out_specs=[vmem(), vmem()],
        scratch_shapes=[pltpu.VMEM((4, 2, ROWS, LANES), jnp.float32), pltpu.SemaphoreType.DMA((4, 2))],
        name="windows",
    )(*arrays)


def both_iterations(table, own, near, far):
    scratch = [
        (PARTS, FRAME1, LANES),
        (2 * KINDS, FRAME1, LANES),
        (2 * KINDS, FRAME1, LANES),
        (FRAME1, LANES),
        (SLICES, FRAME1, LANES),
        (SLICES, FRAME1, LANES),
        (SLICES, FRAME1, LANES),
        (SLICES, FRAME2, LANES),
        (SLICES, FRAME2, LANES),
        (SLICES, FRAME1, LANES),
        (SLICES, FRAME1, LANES),
        (GROUP, K + 1, FRAME1, LANES),
        (GROUP, K + 1, FRAME1, LANES),
        (PAIRS, 2, 9, 8, LANES),
        (PAIRS, 2, 9, 8, LANES),
        (PAIRS, 2, 9, 8, LANES),
        (PAIRS, 2, 9, 8, LANES),
        (PAIRS, 2, 9, 8, LANES),
    ]
    return pl.pallas_call(
        main_kernel,
        out_shape=f32(SLICES, TILE_ROWS, LANES),
        in_specs=[smem(), vmem(), vmem(), vmem()],
        out_specs=vmem(),
        scratch_shapes=[pltpu.VMEM(shape, jnp.float32) for shape in scratch],
        compiler_params=pltpu.CompilerParams(vmem_limit_bytes=32 * 2**20),
        name="both_iterations",
    )(table, own, near, far)


def gathered(received):
    return pl.pallas_call(
        gather_kernel,
        out_shape=[f32(1, ROWS, 512), f32(1, ROWS, 512)],
        in_specs=[vmem()],
        out_specs=[vmem(), vmem()],
        compiler_params=pltpu.CompilerParams(vmem_limit_bytes=2 * 2**20),
        name="gathered",
    )(received)


def toward_own_side(array, distance):
    hops = []
    for c in range(2):
        for space in range(16):
            source = (space + (distance if c else -distance)) % 16
            hops.append((c * 16 + source, c * 16 + space))
    return lax.ppermute(array, ("c", *SPACE), hops)


def on_device(initial_density, terminal_cost, running_cost, discount_rate, slice_steps):
    own, edge = windows(initial_density, terminal_cost, running_cost, discount_rate)
    beside = toward_own_side(own, 1)
    near = lax.all_gather(beside, "c")
    band, _, half, _ = place_of()
    numbers = jnp.arange(SLICES, dtype=jnp.int32)
    ahead = (slice_steps[None, :] < slice_steps[:, None]) | ((slice_steps[None, :] == slice_steps[:, None]) & (numbers[None, :] < numbers[:, None]))
    rank = jnp.sum(ahead.astype(jnp.int32), axis=1)
    edge, rank = lax.optimization_barrier((edge, rank))
    order = jnp.sum(jnp.where(rank[None, :] == numbers[:, None], numbers[None, :], 0), axis=1)
    table = jnp.concatenate([order, slice_steps, jnp.stack([band, half]).astype(jnp.int32)])
    far = toward_own_side(edge, 2)
    message = both_iterations(table, own, near, far)
    received = lax.all_to_all(message, TM, 0, 0, tiled=True)
    return tuple(gathered(received))


def solution(mesh):
    finer = Mesh(mesh.devices.reshape(4, 4, 2, 8, 2), ("zh", "x", "c", "y", "zl"))
    placed = (P(SPACE, None), P(SPACE, None), P(SPACE, None), P(SPACE, None), P())
    return jax.shard_map(
        on_device,
        mesh=finer,
        in_specs=placed,
        out_specs=(P(TM, SPACE, None), P(TM, SPACE, None)),
        check_vma=False,
    )
```

```python
import jax
import jax.numpy as jnp
from jax import lax
from jax.experimental import pallas as pl
from jax.experimental.pallas import tpu as pltpu
from jax.sharding import Mesh
from jax.sharding import PartitionSpec as P


K = 8
SLICES = 32
LEAST = 4
KINDS = K - LEAST + 1
GROUP1 = 16
GROUP2 = 16
GROUP = max(GROUP1, GROUP2)
PAIRS = GROUP // 2
HALF = 64
TM = ("zh", "x", "c")
SPACE = ("y", "zl")

time_step = 0.05
diffusion = 2.0
coupling = 0.1

ROWS = 24
TILE_ROWS = 6
TILE_COLS = 64
LANES = 128
COL_AT = 32
FRAME1 = 80
FRAME2 = 48
TOP = 7
PARTS = 5
EDGED = (1, 2, 3)
SCALE = 16.0


def planes_of(ref, at, start, count):
    return [ref[(*at, pl.ds(start + k, 8, stride=count), slice(None))] for k in range(count)]


def put_planes(ref, at, start, planes):
    count = len(planes)
    for k, plane in enumerate(planes):
        ref[(*at, pl.ds(start + k, 8, stride=count), slice(None))] = plane


def row_above(planes):
    return [pltpu.roll(planes[-1], 1, 0), *planes[:-1]]


def row_below(planes):
    return [*planes[1:], pltpu.roll(planes[0], 7, 0)]


def left(plane):
    return pltpu.roll(plane, 1, 1)


def right(plane):
    return pltpu.roll(plane, LANES - 1, 1)


def lanes_of(shape):
    return lax.broadcasted_iota(jnp.int32, shape, len(shape) - 1)


def paired(a, b):
    first = lanes_of(a.shape) < HALF
    return jnp.where(first, a, pltpu.roll(b, HALF, 1)), jnp.where(first, pltpu.roll(a, HALF, 1), b)


def pair_planes(many_a, many_b):
    both = [paired(a, b) for a, b in zip(many_a, many_b)]
    return [even for even, _ in both], [odd for _, odd in both]


def slope_planes(even, odd, beside=None):
    result = []
    for parity, planes in enumerate((even, odd)):
        up, down = row_above(planes), row_below(planes)
        slopes, sums = [], []
        for k in range(len(planes)):
            if parity == 0:
                west, east = left(odd[k]), odd[k]
                if beside is not None:
                    west = jnp.where(lanes_of(west.shape) % HALF == 0, beside[0][k], west)
            else:
                west, east = even[k], right(even[k])
                if beside is not None:
                    east = jnp.where(lanes_of(east.shape) % HALF == HALF - 1, beside[1][k], east)
            slopes.append((down[k] - up[k], east - west))
            sums.append((up[k] + down[k]) + (west + east))
        result.append((planes, slopes, sums))
    return result


def fine_groups(size, table, values, beside, densities, cost, sources, across, along, value_now, density_now, out_value, out_density, spots):
    (value_at, value_n), (density_at, density_n) = spots
    keep_all, share_all = 1.0 - 4.0 * time_step * diffusion, time_step * diffusion
    costs = pair_planes(cost, cost)
    first = lanes_of((8, LANES)) < HALF

    def group(number, carry):
        own = [table[size * number + h] for h in range(size)]
        trips = [table[SLICES + j] for j in own]
        most = trips[-1]

        def taken(ref, at, n, h):
            return pair_planes(*[planes_of(ref, (own[2 * h + side],), at, n) for side in range(2)])

        def left_at(ref, at, h, both):
            for side, planes in enumerate(pair_planes(*both)):
                put_planes(ref, (own[2 * h + side],), at, planes)

        def weights(h, test):
            on = [test(trips[2 * h + side]) for side in range(2)]
            keep = jnp.where(first, jnp.where(on[0], keep_all, 1.0), jnp.where(on[1], keep_all, 1.0))
            share = jnp.where(first, jnp.where(on[0], share_all, 0.0), jnp.where(on[1], share_all, 0.0))
            return keep, share

        for h in range(size // 2):
            start, held, density = taken(values, value_at, value_n, h), taken(densities, value_at, value_n, h), taken(densities, density_at, density_n, h)
            for parity in range(2):
                for k in range(value_n):
                    value_now[0][h, parity, k] = value_now[1][h, parity, k] = start[parity][k]
                    sources[h, parity, k] = costs[parity][k] + (0.5 / SCALE * coupling) * held[parity][k]
                for k in range(density_n):
                    density_now[0][h, parity, k] = density[parity][k]

        def slopes_of(q, h):
            now = [[value_now[q % 2][h, parity, k] for k in range(value_n)] for parity in range(2)]
            edges = taken(beside, value_at, value_n, h) if q == 0 and beside is not None else None
            result = slope_planes(*now, edges)
            for parity in range(2):
                put_planes(across, (2 * h + parity, q), value_at, [a for a, _ in result[parity][1]])
                put_planes(along, (2 * h + parity, q), value_at, [b for _, b in result[parity][1]])
            return result

        def value_step(q):
            for h in range(size // 2):
                keep, share = keep_all, share_all
                if q < K - LEAST:
                    keep, share = weights(h, lambda count: q >= K - count)
                for parity, (now, slopes, sums) in enumerate(slopes_of(q, h)):
                    for k in range(value_n):
                        a, b = slopes[k]
                        value_now[1 - q % 2][h, parity, k] = keep * now[k] + share * (sums[k] + (sources[h, parity, k] - (a * a + b * b)))

        def density_step(i):
            for h in range(size // 2):
                keep, share = keep_all, share_all
                if i >= LEAST:
                    keep, share = weights(h, lambda count: i < count)
                here, rows, more, less = [], [], [], []
                for parity in range(2):
                    a = planes_of(across, (2 * h + parity, K - i), density_at, density_n)
                    b = planes_of(along, (2 * h + parity, K - i), density_at, density_n)
                    now = [density_now[i % 2][h, parity, k] for k in range(density_n)]
                    twice = [plane + plane for plane in now]
                    flux = [twice[k] * a[k] for k in range(density_n)]
                    below = row_below([now[k] + flux[k] for k in range(density_n)])
                    above = row_above([now[k] - flux[k] for k in range(density_n)])
                    drift = [twice[k] * b[k] for k in range(density_n)]
                    here.append(now)
                    rows.append([below[k] + above[k] for k in range(density_n)])
                    more.append([now[k] + drift[k] for k in range(density_n)])
                    less.append([now[k] - drift[k] for k in range(density_n)])
                for k in range(density_n):
                    around = (rows[0][k] + more[1][k]) + left(less[1][k]), (rows[1][k] + less[0][k]) + right(more[0][k])
                    for parity in range(2):
                        density_now[1 - i % 2][h, parity, k] = keep * here[parity][k] + share * around[parity]

        for q in range(K):
            if q < K - LEAST:
                pl.when(q >= K - most)(lambda q=q: value_step(q))
            else:
                value_step(q)
        for h in range(size // 2):
            left_at(out_value, value_at, h, [planes for planes, _, _ in slopes_of(K, h)])
        for i in range(K):
            if i >= LEAST:
                pl.when(i < most)(lambda i=i: density_step(i))
            else:
                density_step(i)
        for last in range(2):

            @pl.when(most % 2 == last)
            def _(last=last):
                for h in range(size // 2):
                    left_at(out_density, density_at, h, [[density_now[last][h, parity, k] for k in range(density_n)] for parity in range(2)])

        return carry

    lax.fori_loop(0, SLICES // size, group, 0)


def main_kernel(table, own, near, far, message, field, factors, reliefs, cost, m0, u0, e0, m1, u1, fm, fu, across, along, sources, va, vb, da, db):
    band, half = table[2 * SLICES], table[2 * SLICES + 1]
    for position in range(4):

        @pl.when(band == position)
        def _(position=position):
            pieces = [(near, (0,), ROWS, -24), (own, (), ROWS, 0), (near, (1,), ROWS, 24), (far, (), 16, -40 if position < 2 else 48)]
            for ref, at, rows, first in pieces:
                begin = first - TILE_ROWS * position + 40
                low, high = max(begin, TOP), min(begin + rows, FRAME1 - 1)
                for part in range(PARTS):
                    field[part, low:high] = ref[(*at, part, slice(low - begin, high - begin))]

    packed_edges = field[4]
    lane = lanes_of((FRAME1, LANES))
    edges = {}
    for place, part in enumerate(EDGED):
        edges[part] = jnp.where(lane < 64, pltpu.roll(packed_edges, (LANES - place) % LANES, 1), pltpu.roll(packed_edges, place, 1)) if place else packed_edges
    for begin, rate, running in ((0, field[3], field[2]), (KINDS, edges[3], edges[2])):
        quotient = running / rate
        for kind in range(KINDS):
            factor = jnp.exp(rate * (-time_step * (LEAST + kind)))
            factors[begin + kind] = factor
            reliefs[begin + kind] = (1.0 - factor) * quotient * (1.0 / SCALE)
    cost[...] = field[2] * (0.5 / SCALE)

    def opening(j, now):
        density, value, edge = now
        back = SLICES - 1 - j
        m0[j] = density
        u0[back] = value
        e0[back] = edge
        kind = table[SLICES + back] - LEAST
        density = factors[table[SLICES + j] - LEAST] * density
        value = factors[kind] * value + reliefs[kind]
        edge = factors[KINDS + kind] * edge + reliefs[KINDS + kind]
        return density, value, edge

    lax.fori_loop(0, SLICES, opening, (field[0], field[1] * (1.0 / SCALE), edges[1] * (1.0 / SCALE)), unroll=2)

    fine_groups(GROUP1, table, u0, e0, m0, planes_of(cost, (), 7, 9), sources, across, along, (va, vb), (da, db), fu, fm, ((7, 9), (15, 7)))

    inner = pl.ds(16, FRAME2)

    def first_sweep(j, now):
        density, value = now
        back = SLICES - 1 - j
        m1[j] = density
        u1[back] = value
        density = factors[table[SLICES + j] - LEAST, inner] * (density - m0[j, inner]) + fm[j, inner]
        value = factors[table[SLICES + back] - LEAST, inner] * (value - u0[back, inner]) + fu[back, inner]
        return density, value

    lax.fori_loop(0, SLICES, first_sweep, (field[0, inner], field[1, inner] * (1.0 / SCALE)), unroll=4)

    fine_groups(GROUP2, table, u1, None, m1, planes_of(cost, (), 23, 5), sources, across, along, (va, vb), (da, db), fu, fm, ((7, 5), (15, 3)))

    tile, wide = pl.ds(24, 8), pl.ds(40, 8)

    def second_sweep(j, now):
        density, value = now
        back = SLICES - 1 - j
        u0[back, 0:8] = value
        m0[j, 0:8] = density
        density = factors[table[SLICES + j] - LEAST, wide] * (density - m1[j, tile]) + fm[j, tile]
        value = factors[table[SLICES + back] - LEAST, wide] * (value - u1[back, tile]) + fu[back, tile]
        return density, value

    lax.fori_loop(0, SLICES, second_sweep, (field[0, wide], field[1, wide] * (1.0 / SCALE)), unroll=8)

    lane = lanes_of((8, LANES))
    first_half = lane < HALF
    wanted = COL_AT // 2 + lane % HALF // 2 + HALF * (lane % 2)
    for j in range(SLICES):
        density, value = m0[j, 0:8], SCALE * u0[j, 0:8]
        ahead, behind = jnp.where(half == 0, density, value), jnp.where(half == 0, value, density)
        whole = jnp.where(first_half, jnp.take_along_axis(ahead, wanted, 1), jnp.take_along_axis(behind, wanted, 1))
        message[j] = whole[0:TILE_ROWS]


def place_of():
    zh, x, c = (lax.axis_index(axis) for axis in TM)
    return 2 * c + x % 2, 2 * zh + x // 2, x // 2, c


def window_kernel(*refs):
    arrays, (near, far), (blocks, arrived) = refs[:4], refs[4:6], refs[6:]
    _, column, _, core = place_of()
    begin = (column * TILE_COLS + 512 - COL_AT) % 512
    first, shift = begin // LANES, LANES - begin % LANES
    copies = []
    for part, array in enumerate(arrays):
        for which in range(2):
            at = pl.multiple_of(((first + which) % 4) * LANES, LANES)
            copies.append(pltpu.make_async_copy(array.at[:, pl.ds(at, LANES)], blocks.at[part, which], arrived.at[part, which]))
    for copy in copies:
        copy.start()
    lane = lanes_of((ROWS, LANES))
    column_in = lane % HALF * 2 + lane // HALF
    lane_of_it = (column_in + LANES - shift) % LANES
    beside = jnp.zeros((ROWS, LANES), jnp.float32)
    for part in range(PARTS):
        if part < 4:
            for copy in copies[2 * part : 2 * part + 2]:
                copy.wait()
            a, b = blocks[part, 0], blocks[part, 1]
            window = jnp.where(column_in < shift, jnp.take_along_axis(a, lane_of_it, 1), jnp.take_along_axis(b, lane_of_it, 1))
        else:
            window = beside
        near[part] = window

        @pl.when(core == 0)
        def _(window=window, part=part):
            far[part] = window[8:24]

        @pl.when(core != 0)
        def _(window=window, part=part):
            far[part] = window[0:16]

        if part in EDGED:
            place = EDGED.index(part)
            beside = jnp.where(lane == place, pltpu.roll(a, shift + 1 + place, 1), beside)
            beside = jnp.where(lane == LANES - 1 - place, pltpu.roll(b, shift - 1 - place, 1), beside)


def gather_kernel(received, density, value):
    first_half = lanes_of((TILE_ROWS, LANES)) < 64
    for zh in range(4):
        for band in range(4):
            at = [zh * 8 + (2 * half + band % 2) * 2 + band // 2 for half in range(2)]
            a, b = received[at[0]], received[at[1]]
            rows, lanes = slice(TILE_ROWS * band, TILE_ROWS * (band + 1)), slice(LANES * zh, LANES * (zh + 1))
            density[0, rows, lanes] = jnp.where(first_half, a, b)
            value[0, rows, lanes] = pltpu.roll(jnp.where(first_half, b, a), 64, 1)


def vmem():
    return pl.BlockSpec(memory_space=pltpu.VMEM)


def smem():
    return pl.BlockSpec(memory_space=pltpu.SMEM)


def f32(*shape):
    return jax.ShapeDtypeStruct(shape, jnp.float32)


def windows(*arrays):
    return pl.pallas_call(
        window_kernel,
        out_shape=[f32(PARTS, ROWS, LANES), f32(PARTS, 16, LANES)],
        in_specs=[pl.BlockSpec(memory_space=pl.ANY)] * 4,
        out_specs=[vmem(), vmem()],
        scratch_shapes=[pltpu.VMEM((4, 2, ROWS, LANES), jnp.float32), pltpu.SemaphoreType.DMA((4, 2))],
        name="windows",
    )(*arrays)


def both_iterations(table, own, near, far):
    scratch = [
        (PARTS, FRAME1, LANES),
        (2 * KINDS, FRAME1, LANES),
        (2 * KINDS, FRAME1, LANES),
        (FRAME1, LANES),
        (SLICES, FRAME1, LANES),
        (SLICES, FRAME1, LANES),
        (SLICES, FRAME1, LANES),
        (SLICES, FRAME2, LANES),
        (SLICES, FRAME2, LANES),
        (SLICES, FRAME1, LANES),
        (SLICES, FRAME1, LANES),
        (GROUP, K + 1, FRAME1, LANES),
        (GROUP, K + 1, FRAME1, LANES),
        (PAIRS, 2, 9, 8, LANES),
        (PAIRS, 2, 9, 8, LANES),
        (PAIRS, 2, 9, 8, LANES),
        (PAIRS, 2, 9, 8, LANES),
        (PAIRS, 2, 9, 8, LANES),
    ]
    return pl.pallas_call(
        main_kernel,
        out_shape=f32(SLICES, TILE_ROWS, LANES),
        in_specs=[smem(), vmem(), vmem(), vmem()],
        out_specs=vmem(),
        scratch_shapes=[pltpu.VMEM(shape, jnp.float32) for shape in scratch],
        compiler_params=pltpu.CompilerParams(vmem_limit_bytes=32 * 2**20),
        name="both_iterations",
    )(table, own, near, far)


def gathered(received):
    return pl.pallas_call(
        gather_kernel,
        out_shape=[f32(1, ROWS, 512), f32(1, ROWS, 512)],
        in_specs=[vmem()],
        out_specs=[vmem(), vmem()],
        compiler_params=pltpu.CompilerParams(vmem_limit_bytes=2 * 2**20),
        name="gathered",
    )(received)


def toward_own_side(array, distance):
    hops = []
    for c in range(2):
        for space in range(16):
            source = (space + (distance if c else -distance)) % 16
            hops.append((c * 16 + source, c * 16 + space))
    return lax.ppermute(array, ("c", *SPACE), hops)


def on_device(initial_density, terminal_cost, running_cost, discount_rate, slice_steps):
    own, edge = windows(initial_density, terminal_cost, running_cost, discount_rate)
    beside = toward_own_side(own, 1)
    near = lax.all_gather(beside, "c")
    band, _, half, _ = place_of()
    numbers = jnp.arange(SLICES, dtype=jnp.int32)
    ahead = (slice_steps[None, :] < slice_steps[:, None]) | ((slice_steps[None, :] == slice_steps[:, None]) & (numbers[None, :] < numbers[:, None]))
    rank = jnp.sum(ahead.astype(jnp.int32), axis=1)
    order = jnp.sum(jnp.where(rank[None, :] == numbers[:, None], numbers[None, :], 0), axis=1)
    table = jnp.concatenate([order, slice_steps, jnp.stack([band, half]).astype(jnp.int32)])
    edge, table = lax.optimization_barrier((edge, table))
    far = toward_own_side(edge, 2)
    message = both_iterations(table, own, near, far)
    received = lax.all_to_all(message, TM, 0, 0, tiled=True)
    return tuple(gathered(received))


def solution(mesh):
    finer = Mesh(mesh.devices.reshape(4, 4, 2, 8, 2), ("zh", "x", "c", "y", "zl"))
    placed = (P(SPACE, None), P(SPACE, None), P(SPACE, None), P(SPACE, None), P())
    return jax.shard_map(
        on_device,
        mesh=finer,
        in_specs=placed,
        out_specs=(P(TM, SPACE, None), P(TM, SPACE, None)),
        check_vma=False,
    )
```
